32 devices in a mesh: grp: 4 (over z), dev: 8 (over y, x, core).
Axes of the slice: x: 2, y: 2, z: 4, core: 2. Of those that a mesh axis runs over, the one named last changes fastest.
Arguments:
- feats: bfloat16 [96, 3200], P(('grp', 'dev')), may hold values from -6 to 6
- ln_gain: float32 [3200], replicated, may hold values from 0.1 to 1.9
- ln_shift: float32 [3200], replicated, may hold values from -3 to 3
- w_proj: bfloat16 [3200, 8192], P(None, 'dev'), may hold values from -0.109375 to 0.109375
- b_proj: float32 [8192], P('dev'), may hold values from -3 to 3
- cotangent: bfloat16 [96, 8192], P('grp', 'dev'), may hold values from -6 to 6
- img_seq: int32 [32], replicated, may hold values from 0 to 3, as said below
- img_count: int32 [32], replicated, may hold values from 1 to 5, as said below
- img_offset: int32 [32], replicated, may hold values from 0 to 23, as said below
Outputs:
- projected: bfloat16 [96, 8192], P('grp', 'dev')
- grad_feats: bfloat16 [96, 3200], P(('grp', 'dev'))
- grad_weight: float32 [3200, 8192], P(None, 'dev')
- grad_bias: float32 [8192], P('dev')
The draws below stay inside these ranges and needn't reach their ends.
Inputs may be any that keep to these rules, and one draw needn't show every extreme that they name: Image i is sent to sequence img_seq[i], which fills rows img_seq[i] * 24 to img_seq[i] * 24 + 23 of projected. Of the 24 encoder rows of each group, exactly 6 go to each sequence. `img_count`: the counts add up to 96; no image spans the rows of two groups. `img_offset`: the images of one sequence cover its 24 rows exactly once.
All inputs are finite; a program needn't handle non-finite values.
Results may differ from the reference program's by a relative error of at most 0.0075.
Values may be sent and summed in bfloat16 or wider, within the bound.
No kernel may reach another device: no remote copies, remote signals or barrier semaphores. Data moves between devices by JAX's collectives and lax.ppermute only.
A program may use at most 128 MiB of HBM per device.

```python
import jax
import jax.numpy as jnp
from jax import lax

D_VIS = 3200
D_LLM = 8192
GROUP_ROWS = 24
PAIR_ROWS = 6
ENC_ROWS = 96
IMAGES = 32
N_GRP = 4


def draw_order(sub_key):
    return jax.random.permutation(sub_key, 2 * N_GRP)


def image_plan(key):
    key_sizes, key_order, key_slots = jax.random.split(jax.random.fold_in(key, 31), 3)
    first_part = jax.random.randint(key_sizes, (N_GRP, N_GRP), 1, PAIR_ROWS)
    counts = jnp.stack([first_part, PAIR_ROWS - first_part], axis=-1).reshape(N_GRP, 2 * N_GRP)
    targets = jnp.broadcast_to(jnp.arange(N_GRP, dtype=jnp.int32)[None, :, None], (N_GRP, N_GRP, 2)).reshape(N_GRP, 2 * N_GRP)
    shuffles = jax.vmap(draw_order)(jax.random.split(key_order, N_GRP))
    counts = jnp.take_along_axis(counts, shuffles, axis=1).reshape(IMAGES)
    targets = jnp.take_along_axis(targets, shuffles, axis=1).reshape(IMAGES)
    priority = jax.random.permutation(key_slots, IMAGES)
    earlier = (targets[None, :] == targets[:, None]) & (priority[None, :] < priority[:, None])
    offsets = jnp.sum(jnp.where(earlier, counts[None, :], 0), axis=1)
    return (targets.astype(jnp.int32), counts.astype(jnp.int32), offsets.astype(jnp.int32))


def draw_img_seq(key, part):
    return image_plan(key)[0]


def draw_img_count(key, part):
    return image_plan(key)[1]


def draw_img_offset(key, part):
    return image_plan(key)[2]


def level_of(key, extent, cuts, least, high):
    factor_of = 1.0
    for position, parts in cuts:
        steps = jax.random.uniform(jax.random.fold_in(jax.random.fold_in(key, 6), position), (parts,), jnp.float32, least / len(cuts), high / len(cuts))
        factor_of = factor_of * jnp.repeat(jnp.exp(steps), extent[position] // parts).reshape((-1,) + (1,) * (len(extent) - 1 - position))
    return factor_of


def bell_draw(stream_key, extent, width, bound, shards=(), kind=jnp.bfloat16):
    entries = width * jax.random.normal(stream_key, extent, jnp.float32)
    if shards:
        entries = entries * level_of(stream_key, extent, shards, -0.22, 0.18)
    return jnp.clip(entries, -bound, bound).astype(kind)


def setup_inputs(seed: int = 0) -> dict:
    seeds = jax.random.split(jax.random.key(seed), 10)
    feats = bell_draw(seeds[0], (ENC_ROWS, D_VIS), 1.0, 6.0, ((0, 32),))
    ln_gain = jnp.clip(1.0 + 0.18 * jax.random.normal(seeds[1], (D_VIS,), jnp.float32), 0.1, 1.9)
    ln_shift = bell_draw(seeds[2], (D_VIS,), 0.5, 3.0, (), jnp.float32)
    w_proj = bell_draw(seeds[3], (D_VIS, D_LLM), D_VIS ** -0.5, 0.109375, ((1, 8),))
    b_proj = bell_draw(seeds[4], (D_LLM,), 0.5, 3.0, ((0, 8),), jnp.float32)
    cotangent = bell_draw(seeds[5], (ENC_ROWS, D_LLM), 1.0, 6.0, ((0, 4), (1, 8)))
    img_seq = draw_img_seq(jax.random.fold_in(seeds[9], 71), 0)
    img_count = draw_img_count(jax.random.fold_in(seeds[9], 71), 0)
    img_offset = draw_img_offset(jax.random.fold_in(seeds[9], 71), 0)
    return dict(feats=feats, ln_gain=ln_gain, ln_shift=ln_shift, w_proj=w_proj, b_proj=b_proj, cotangent=cotangent, img_seq=img_seq, img_count=img_count, img_offset=img_offset)


epsilon = 1e-05

def activate(values):
    return jax.nn.gelu(values, approximate=True)

def row_targets(img_seq, img_count, img_offset, all_rows, seq_rows):
    img_ends = jnp.cumsum(img_count).astype(jnp.int32)
    img_starts = img_ends - img_count
    row_ids = jnp.arange(all_rows, dtype=jnp.int32)
    member = ((row_ids[:, None] >= img_starts[None, :]) & (row_ids[:, None] < img_ends[None, :])).astype(jnp.int32)
    base_rows = img_seq * seq_rows + img_offset - img_starts
    return (lax.optimization_barrier(jnp.sum(member * base_rows[None, :], axis=1)) + row_ids).astype(jnp.int32)

def normalize(rows, ln_gain, ln_shift):
    values = rows.astype(jnp.float32)
    row_mean = lax.optimization_barrier(jnp.mean(values, axis=1, keepdims=True))
    centered = values - row_mean
    inv_scale = lax.rsqrt(lax.optimization_barrier(jnp.mean(centered * centered, axis=1, keepdims=True)) + epsilon)
    unit_rows = centered * inv_scale
    return (unit_rows, inv_scale, unit_rows * ln_gain + ln_shift)

def reference(feats, ln_gain, ln_shift, w_proj, b_proj, cotangent, img_seq, img_count, img_offset):
    all_rows = feats.shape[0]
    target = row_targets(img_seq, img_count, img_offset, all_rows, GROUP_ROWS)
    unit_rows, inv_scale, normed = normalize(feats, ln_gain, ln_shift)
    normed = normed.astype(jnp.bfloat16)
    pre_act = jnp.dot(normed, w_proj, preferred_element_type=jnp.float32) + b_proj
    acted, gelu_pull = jax.vjp(activate, pre_act)
    projected = jnp.zeros((all_rows, w_proj.shape[1]), jnp.bfloat16).at[target].set(acted.astype(jnp.bfloat16))
    upstream = cotangent[target].astype(jnp.float32)
    grad_pre = gelu_pull(upstream)[0].astype(jnp.bfloat16)
    grad_weight = jnp.dot(normed.T, grad_pre, preferred_element_type=jnp.float32)
    grad_bias = lax.optimization_barrier(jnp.sum(grad_pre.astype(jnp.float32), axis=0))
    grad_normed = jnp.dot(grad_pre, w_proj.T, preferred_element_type=jnp.float32)
    scaled_grad = grad_normed * ln_gain
    grad_feats = inv_scale * (scaled_grad - lax.optimization_barrier(jnp.mean(scaled_grad, axis=1, keepdims=True)) - unit_rows * lax.optimization_barrier(jnp.mean(scaled_grad * unit_rows, axis=1, keepdims=True)))
    return (projected, grad_feats.astype(jnp.bfloat16), grad_weight, grad_bias)
```

```python
import jax
import jax.numpy as jnp
from jax import lax
from jax.sharding import PartitionSpec as P

epsilon = 1e-05


def activate(values):
    return jax.nn.gelu(values, approximate=True)


def row_targets(img_seq, img_count, img_offset, all_rows, seq_rows):
    image_ids = jnp.arange(img_count.shape[0], dtype=jnp.int32)
    img_starts = jnp.sum(
        jnp.where(image_ids[None, :] < image_ids[:, None], img_count[None, :], 0), axis=1
    )
    img_ends = img_starts + img_count
    row_ids = jnp.arange(all_rows, dtype=jnp.int32)
    member = (
        (row_ids[:, None] >= img_starts[None, :]) & (row_ids[:, None] < img_ends[None, :])
    ).astype(jnp.int32)
    base_rows = img_seq * seq_rows + img_offset - img_starts
    return jnp.sum(member * base_rows[None, :], axis=1) + row_ids


def normalize(rows, ln_gain, ln_shift):
    values = rows.astype(jnp.float32)
    row_mean = jnp.mean(values, axis=1, keepdims=True)
    centered = values - row_mean
    inv_scale = lax.rsqrt(jnp.mean(centered * centered, axis=1, keepdims=True) + epsilon)
    unit_rows = centered * inv_scale
    return (unit_rows, inv_scale, unit_rows * ln_gain + ln_shift)


def local(feats, ln_gain, ln_shift, w_proj, b_proj, cotangent, img_seq, img_count, img_offset):
    lane_count = lax.axis_size("dev")
    groups = lax.axis_size("grp")
    my_group = lax.axis_index("grp")
    own_rows = feats.shape[0]
    group_rows = own_rows * lane_count
    all_rows = group_rows * groups
    row_base = my_group * group_rows
    target = row_targets(img_seq, img_count, img_offset, all_rows, group_rows)
    source_rows = (
        jnp.zeros((all_rows,), jnp.int32).at[target].set(jnp.arange(all_rows, dtype=jnp.int32))
    )
    arrivals = lax.dynamic_slice_in_dim(source_rows, row_base, group_rows)
    whole = lax.all_gather(feats, "dev", axis=0, tiled=True)
    unit_rows, inv_scale, normed = normalize(whole, ln_gain, ln_shift)
    normed = normed.astype(jnp.bfloat16)
    pre_act = jnp.dot(normed, w_proj, preferred_element_type=jnp.float32) + b_proj
    acted, gelu_pull = jax.vjp(activate, pre_act)
    local_cols = acted.astype(jnp.bfloat16)
    all_cols = lax.all_gather(local_cols, "grp", axis=0, tiled=True)
    projected = all_cols[arrivals]
    all_grads = lax.all_gather(cotangent, "grp", axis=0, tiled=True)
    own_targets = lax.dynamic_slice_in_dim(target, row_base, group_rows)
    upstream = all_grads[own_targets]
    grad_pre = gelu_pull(upstream.astype(jnp.float32))[0].astype(jnp.bfloat16)
    weight_term = lax.dot_general(
        normed, grad_pre, (((0,), (0,)), ((), ())), preferred_element_type=jnp.float32
    )
    bias_term = jnp.sum(grad_pre.astype(jnp.float32), axis=0)
    vis_width = weight_term.shape[0]
    padded_rows = (vis_width + groups) // groups * groups
    joint_term = jnp.concatenate(
        [
            weight_term,
            bias_term[None, :],
            jnp.zeros((padded_rows - vis_width - 1, weight_term.shape[1]), jnp.float32),
        ],
        axis=0,
    )
    summed_share = lax.psum_scatter(joint_term, "grp", scatter_dimension=0, tiled=True)
    summed_whole = lax.all_gather(
        summed_share.astype(jnp.bfloat16), "grp", axis=0, tiled=True
    ).astype(summed_share.dtype)
    grad_weight = summed_whole[:vis_width]
    grad_bias = summed_whole[vis_width]
    grad_normed = lax.psum_scatter(
        lax.dot_general(
            grad_pre, w_proj, (((1,), (1,)), ((), ())), preferred_element_type=jnp.float32
        ),
        "dev",
        scatter_dimension=0,
        tiled=True,
    )
    lane_start = lax.axis_index("dev") * own_rows
    own_unit = lax.dynamic_slice_in_dim(unit_rows, lane_start, own_rows, 0)
    own_scale = lax.dynamic_slice_in_dim(inv_scale, lane_start, own_rows, 0)
    scaled_grad = grad_normed * ln_gain
    grad_feats = own_scale * (
        scaled_grad
        - jnp.mean(scaled_grad, axis=1, keepdims=True)
        - own_unit * jnp.mean(scaled_grad * own_unit, axis=1, keepdims=True)
    )
    return (projected, grad_feats.astype(jnp.bfloat16), grad_weight, grad_bias)


def solution(mesh):
    placed = (
        P(("grp", "dev"), None),
        P(),
        P(),
        P(None, "dev"),
        P("dev"),
        P("grp", "dev"),
        P(),
        P(),
        P(),
    )
    return jax.shard_map(
        local,
        mesh=mesh,
        in_specs=placed,
        out_specs=(P("grp", "dev"), P(("grp", "dev"), None), P(None, "dev"), P("dev")),
        check_vma=False,
    )
```

```python
import jax
import jax.numpy as jnp
from jax import lax
from jax.sharding import PartitionSpec as P

epsilon = 1e-05
root_two_over_pi = 0.7978845608028654
cubic = 0.044715


def row_targets(img_seq, img_count, img_offset, all_rows, seq_rows):
    image_ids = jnp.arange(img_count.shape[0], dtype=jnp.int32)
    img_starts = jnp.sum(
        jnp.where(image_ids[None, :] < image_ids[:, None], img_count[None, :], 0), axis=1
    )
    img_ends = img_starts + img_count
    row_ids = jnp.arange(all_rows, dtype=jnp.int32)
    member = (
        (row_ids[:, None] >= img_starts[None, :]) & (row_ids[:, None] < img_ends[None, :])
    ).astype(jnp.int32)
    base_rows = img_seq * seq_rows + img_offset - img_starts
    return jnp.sum(member * base_rows[None, :], axis=1) + row_ids


def normalize(rows, ln_gain, ln_shift):
    values = rows.astype(jnp.float32)
    row_mean = jnp.mean(values, axis=1, keepdims=True)
    centered = values - row_mean
    inv_scale = lax.rsqrt(jnp.mean(centered * centered, axis=1, keepdims=True) + epsilon)
    unit_rows = centered * inv_scale
    return (unit_rows, inv_scale, unit_rows * ln_gain + ln_shift)


def gelu_and_slope(values):
    square = values * values
    bent = jnp.tanh(root_two_over_pi * values * (1.0 + cubic * square))
    half = 0.5 * (1.0 + bent)
    slope = half + 0.5 * values * (1.0 - bent * bent) * (
        root_two_over_pi * (1.0 + 3.0 * cubic * square)
    )
    return values * half, slope


def gather_groups(block):
    groups = lax.axis_size("grp")
    if groups & (groups - 1):
        return lax.all_gather(block, "grp", axis=0), jnp.arange(groups, dtype=jnp.int32)
    held = block[None]
    step = 1
    while step < groups:
        pairs = [(group, group ^ step) for group in range(groups)]
        held = jnp.concatenate([held, lax.ppermute(held, "grp", pairs)], axis=0)
        step *= 2
    return held, lax.axis_index("grp") ^ jnp.arange(groups, dtype=jnp.int32)


def backward_norm(grad_normed, ln_gain, unit_rows, inv_scale):
    scaled_grad = grad_normed * ln_gain
    grad_feats = inv_scale * (
        scaled_grad
        - jnp.mean(scaled_grad, axis=1, keepdims=True)
        - unit_rows * jnp.mean(scaled_grad * unit_rows, axis=1, keepdims=True)
    )
    return grad_feats.astype(jnp.bfloat16)


def gathered_plan(feats, ln_gain, ln_shift, w_proj, b_proj, cotangent, img_seq, img_count, img_offset):
    lanes = lax.axis_size("dev")
    groups = lax.axis_size("grp")
    my_group = lax.axis_index("grp")
    own_rows, vis_width = feats.shape
    group_rows = own_rows * lanes
    all_rows = group_rows * groups
    unit_rows, inv_scale, normed = normalize(feats, ln_gain, ln_shift)
    column, group_of = gather_groups(normed.astype(jnp.bfloat16))
    grads, _ = gather_groups(cotangent)
    rows = lax.all_gather(column, "dev", axis=0).reshape(all_rows, vis_width)
    within = jnp.arange(lanes, dtype=jnp.int32)[:, None] * own_rows + jnp.arange(own_rows, dtype=jnp.int32)
    slot_rows = (group_of[None, :, None] * group_rows + within[:, None, :]).reshape(all_rows)
    seq_rows = (
        group_of[:, None] * group_rows + jnp.arange(group_rows, dtype=jnp.int32)[None, :]
    ).reshape(all_rows)
    target = row_targets(img_seq, img_count, img_offset, all_rows, group_rows)
    slot_target = target[slot_rows]
    pre_act = jnp.dot(rows, w_proj, preferred_element_type=jnp.float32) + b_proj
    acted, slope = gelu_and_slope(pre_act)
    arrivals = slot_target[None, :] == (
        my_group * group_rows + jnp.arange(group_rows, dtype=jnp.int32)
    )[:, None]
    projected = jnp.dot(
        arrivals.astype(jnp.bfloat16), acted.astype(jnp.bfloat16), preferred_element_type=jnp.float32
    ).astype(jnp.bfloat16)
    sources = slot_target[:, None] == seq_rows[None, :]
    upstream = jnp.dot(
        sources.astype(jnp.bfloat16),
        grads.reshape(all_rows, grads.shape[2]),
        preferred_element_type=jnp.float32,
    )
    grad_pre = (upstream * slope).astype(jnp.bfloat16)
    grad_weight = lax.dot_general(
        rows, grad_pre, (((0,), (0,)), ((), ())), preferred_element_type=jnp.float32
    )
    grad_bias = jnp.sum(grad_pre.astype(jnp.float32), axis=0)
    is_own = (slot_rows // group_rows)[None, :] == my_group
    mine = (slot_rows % group_rows)[None, :] == jnp.arange(group_rows, dtype=jnp.int32)[:, None]
    own_pre = jnp.dot(
        (is_own & mine).astype(jnp.bfloat16), grad_pre, preferred_element_type=jnp.float32
    ).astype(jnp.bfloat16)
    terms = lax.dot_general(
        own_pre, w_proj, (((1,), (1,)), ((), ())), preferred_element_type=jnp.float32
    ).reshape(lanes, own_rows, vis_width)
    swapped = lax.all_to_all(terms.astype(jnp.bfloat16), "dev", 0, 0)
    grad_normed = jnp.sum(swapped.astype(jnp.float32), axis=0)
    grad_feats = backward_norm(grad_normed, ln_gain, unit_rows, inv_scale)
    return (projected, grad_feats, grad_weight, grad_bias)


def summed_plan(feats, ln_gain, ln_shift, w_proj, b_proj, cotangent, img_seq, img_count, img_offset):
    lane_count = lax.axis_size("dev")
    groups = lax.axis_size("grp")
    my_group = lax.axis_index("grp")
    own_rows = feats.shape[0]
    group_rows = own_rows * lane_count
    all_rows = group_rows * groups
    row_base = my_group * group_rows
    target = row_targets(img_seq, img_count, img_offset, all_rows, group_rows)
    source_rows = (
        jnp.zeros((all_rows,), jnp.int32).at[target].set(jnp.arange(all_rows, dtype=jnp.int32))
    )
    arrivals = lax.dynamic_slice_in_dim(source_rows, row_base, group_rows)
    whole = lax.all_gather(feats, "dev", axis=0, tiled=True)
    unit_rows, inv_scale, normed = normalize(whole, ln_gain, ln_shift)
    normed = normed.astype(jnp.bfloat16)
    pre_act = jnp.dot(normed, w_proj, preferred_element_type=jnp.float32) + b_proj
    acted, slope = gelu_and_slope(pre_act)
    local_cols = acted.astype(jnp.bfloat16)
    all_cols = lax.all_gather(local_cols, "grp", axis=0, tiled=True)
    projected = all_cols[arrivals]
    all_grads = lax.all_gather(cotangent, "grp", axis=0, tiled=True)
    own_targets = lax.dynamic_slice_in_dim(target, row_base, group_rows)
    upstream = all_grads[own_targets]
    grad_pre = (upstream.astype(jnp.float32) * slope).astype(jnp.bfloat16)
    weight_term = lax.dot_general(
        normed, grad_pre, (((0,), (0,)), ((), ())), preferred_element_type=jnp.float32
    )
    bias_term = jnp.sum(grad_pre.astype(jnp.float32), axis=0)
    vis_width = weight_term.shape[0]
    padded_rows = (vis_width + groups) // groups * groups
    joint_term = jnp.concatenate(
        [
            weight_term,
            bias_term[None, :],
            jnp.zeros((padded_rows - vis_width - 1, weight_term.shape[1]), jnp.float32),
        ],
        axis=0,
    )
    summed_share = lax.psum_scatter(joint_term, "grp", scatter_dimension=0, tiled=True)
    summed_whole = lax.all_gather(
        summed_share.astype(jnp.bfloat16), "grp", axis=0, tiled=True
    ).astype(summed_share.dtype)
    grad_weight = summed_whole[:vis_width]
    grad_bias = summed_whole[vis_width]
    grad_normed = lax.psum_scatter(
        lax.dot_general(
            grad_pre, w_proj, (((1,), (1,)), ((), ())), preferred_element_type=jnp.float32
        ),
        "dev",
        scatter_dimension=0,
        tiled=True,
    )
    lane_start = lax.axis_index("dev") * own_rows
    own_unit = lax.dynamic_slice_in_dim(unit_rows, lane_start, own_rows, 0)
    own_scale = lax.dynamic_slice_in_dim(inv_scale, lane_start, own_rows, 0)
    grad_feats = backward_norm(grad_normed, ln_gain, own_unit, own_scale)
    return (projected, grad_feats, grad_weight, grad_bias)


def local(*arrays):
    feats, w_proj = arrays[0], arrays[3]
    all_rows = feats.shape[0] * lax.axis_size("dev") * lax.axis_size("grp")
    if all_rows * jnp.dtype(jnp.bfloat16).itemsize <= w_proj.shape[1] * jnp.dtype(jnp.float32).itemsize:
        return gathered_plan(*arrays)
    return summed_plan(*arrays)


def solution(mesh):
    placed = (
        P(("grp", "dev"), None),
        P(),
        P(),
        P(None, "dev"),
        P("dev"),
        P("grp", "dev"),
        P(),
        P(),
        P(),
    )
    return jax.shard_map(
        local,
        mesh=mesh,
        in_specs=placed,
        out_specs=(P("grp", "dev"), P(("grp", "dev"), None), P(None, "dev"), P("dev")),
        check_vma=False,
    )
```

```python
import functools

import jax
import jax.numpy as jnp
from jax import lax
from jax.experimental import pallas as pl
from jax.experimental.pallas import tpu as pltpu
from jax.sharding import PartitionSpec as P

epsilon = 1e-05
root_two_over_pi = 0.7978845608028654
cubic = 0.044715
MIB = 1 << 20
WHOLE = pl.BlockSpec(memory_space=pltpu.VMEM)
SCALARS = pl.BlockSpec(memory_space=pltpu.SMEM)
LEFT = pl.BlockSpec(memory_space=pl.ANY)


def row_targets(img_seq, img_count, img_offset, all_rows, seq_rows):
    image_ids = jnp.arange(img_count.shape[0], dtype=jnp.int32)
    img_starts = jnp.sum(
        jnp.where(image_ids[None, :] < image_ids[:, None], img_count[None, :], 0), axis=1
    )
    img_ends = img_starts + img_count
    row_ids = jnp.arange(all_rows, dtype=jnp.int32)
    member = (
        (row_ids[:, None] >= img_starts[None, :]) & (row_ids[:, None] < img_ends[None, :])
    ).astype(jnp.int32)
    base_rows = img_seq * seq_rows + img_offset - img_starts
    return jnp.sum(member * base_rows[None, :], axis=1) + row_ids


def normalize(rows, ln_gain, ln_shift):
    values = rows.astype(jnp.float32)
    row_mean = jnp.mean(values, axis=1, keepdims=True)
    centered = values - row_mean
    inv_scale = lax.rsqrt(jnp.mean(centered * centered, axis=1, keepdims=True) + epsilon)
    unit_rows = centered * inv_scale
    return (unit_rows, inv_scale, unit_rows * ln_gain + ln_shift)


def gelu_and_slope(values):
    square = values * values
    bent = jnp.tanh(root_two_over_pi * values * (1.0 + cubic * square))
    half = 0.5 * (1.0 + bent)
    slope = half + 0.5 * values * (1.0 - bent * bent) * (
        root_two_over_pi * (1.0 + 3.0 * cubic * square)
    )
    return values * half, slope


def backward_norm(grad_normed, ln_gain, unit_rows, inv_scale):
    scaled_grad = grad_normed * ln_gain
    grad_feats = inv_scale * (
        scaled_grad
        - jnp.mean(scaled_grad, axis=1, keepdims=True)
        - unit_rows * jnp.mean(scaled_grad * unit_rows, axis=1, keepdims=True)
    )
    return grad_feats.astype(jnp.bfloat16)


def norm_pack_kernel(block, feats, gain, shift, cotangent, packed):
    own_rows, vis_width = feats.shape
    units = cotangent.shape[1]
    normed = normalize(feats[...], gain[...], shift[...])[2]
    if block > own_rows:
        normed = jnp.concatenate([normed, jnp.zeros((block - own_rows, vis_width), jnp.float32)], axis=0)
    pieces = []
    for first in range(0, vis_width, units):
        piece = normed[:, first : first + units]
        if piece.shape[1] < units:
            piece = jnp.concatenate([piece, jnp.zeros((block, units - piece.shape[1]), jnp.float32)], axis=1)
        pieces.append(piece)
    count = len(pieces) * block
    packed[:count, :] = jnp.concatenate(pieces, axis=0).astype(jnp.bfloat16)
    packed[count:, :] = cotangent[...]


def unpack_kernel(block, *refs):
    sources, (column, grads) = refs[:-2], refs[-2:]
    vis_width, units = column.shape[1], grads.shape[1]
    parts = [source[place] for source in sources for place in range(source.shape[0])]
    count = (vis_width + units - 1) // units * block
    seq_rows = parts[0].shape[0] - count
    for at, first in enumerate(range(0, vis_width, units)):
        width = min(units, vis_width - first)
        piece = jnp.concatenate(
            [part[at * block : (at + 1) * block, :width].astype(jnp.float32) for part in parts], axis=0
        )
        column[:, first : first + width] = piece.astype(jnp.bfloat16)
    for at, part in enumerate(parts):
        grads[at * seq_rows : (at + 1) * seq_rows, :] = part[count:, :]


def slot_targets(my_group, block, own_rows, lanes, groups, img_seq, img_count, img_offset):
    group_rows = own_rows * lanes
    slots = lax.broadcasted_iota(jnp.int32, (1, lanes * groups * block), 1)
    within = slots & (block - 1)
    row_ids = (
        (my_group ^ ((slots // block) & (groups - 1))) * group_rows
        + slots // (block * groups) * own_rows
        + within
    )
    target = jnp.zeros_like(row_ids)
    start = jnp.int32(0)
    for image in range(img_seq.shape[0]):
        end = start + img_count[image]
        member = (row_ids >= start) & (row_ids < end)
        base = img_seq[image] * group_rows + img_offset[image] - start
        target = jnp.where(member, row_ids + base, target)
        start = end
    return jnp.where(within < own_rows, target, -1)


def fused_kernel(
    block, own_rows, lanes, groups, width,
    place, img_seq, img_count, img_offset, rows, grads, bias, w_far,
    projected, grad_bias, grad_pre, terms, w_near, total, arrived,
):
    units = w_far.shape[1]
    steps = units // width
    copies = [
        pltpu.make_async_copy(w_far.at[:, pl.ds(step * width, width)], w_near.at[step], arrived.at[step])
        for step in range(steps)
    ]
    for copy in copies:
        copy.start()
    group_rows = own_rows * lanes
    all_rows = group_rows * groups
    slot_count = lanes * groups * block
    my_group = place[0]
    target = slot_targets(my_group, block, own_rows, lanes, groups, img_seq, img_count, img_offset)
    places = lax.broadcasted_iota(jnp.int32, (all_rows, slot_count), 0)
    distance = places // group_rows
    seq_rows = places - distance * group_rows + (my_group ^ distance) * group_rows
    routes = (target == seq_rows).astype(jnp.float32)
    arrivals = routes[:group_rows].astype(jnp.bfloat16)
    sources = routes.T.astype(jnp.bfloat16)
    own_place = lax.broadcasted_iota(jnp.int32, (lanes * block, slot_count), 0)
    own_slot = lax.broadcasted_iota(jnp.int32, (lanes * block, slot_count), 1)
    keep = own_slot == own_place // block * (block * groups) + (own_place & (block - 1))
    keep = keep.astype(jnp.float32).astype(jnp.bfloat16)
    for step in range(steps):
        copies[step].wait()
        span = slice(step * width, (step + 1) * width)
        weights = w_near[step]
        pre_act = jnp.dot(rows[...], weights, preferred_element_type=jnp.float32) + bias[:, span]
        acted, slope = gelu_and_slope(pre_act)
        projected[:, span] = jnp.dot(
            arrivals, acted.astype(jnp.bfloat16), preferred_element_type=jnp.float32
        ).astype(jnp.bfloat16)
        upstream = jnp.dot(sources, grads[:, span], preferred_element_type=jnp.float32)
        pulled = (upstream * slope).astype(jnp.bfloat16)
        grad_pre[:, span] = pulled
        grad_bias[:, span] = jnp.sum(pulled.astype(jnp.float32), axis=0, keepdims=True)
        own = jnp.dot(keep, pulled, preferred_element_type=jnp.float32).astype(jnp.bfloat16)
        term = lax.dot_general(own, weights, (((1,), (1,)), ((), ())), preferred_element_type=jnp.float32)
        if step:
            term = total[...] + term
        if step + 1 < steps:
            total[...] = term
        else:
            terms[...] = term.astype(jnp.bfloat16)


def grad_weight_kernel(height, rows, grad_pre, far, near, left):
    copies = []
    for step in range(rows.shape[1] // height):
        span = slice(step * height, (step + 1) * height)
        near[span, :] = lax.dot_general(
            rows[:, span], grad_pre[...], (((0,), (0,)), ((), ())), preferred_element_type=jnp.float32
        )
        copies.append(pltpu.make_async_copy(near.at[span], far.at[span], left.at[step]))
        copies[-1].start()
    for copy in copies:
        copy.wait()


def gathered_plan(feats, ln_gain, ln_shift, w_proj, b_proj, cotangent, img_seq, img_count, img_offset):
    lanes = lax.axis_size("dev")
    groups = lax.axis_size("grp")
    my_group = lax.axis_index("grp")
    own_rows, vis_width = feats.shape
    units = w_proj.shape[1]
    group_rows = own_rows * lanes
    all_rows = group_rows * groups
    block = pl.next_power_of_2(own_rows)
    slot_count = lanes * groups * block
    bfloat16, float32 = jnp.bfloat16, jnp.float32
    packed_rows = pl.cdiv(vis_width, units) * block + group_rows
    held = pl.pallas_call(
        functools.partial(norm_pack_kernel, block),
        out_shape=jax.ShapeDtypeStruct((packed_rows, units), bfloat16),
        in_specs=[WHOLE] * 4,
        out_specs=WHOLE,
        compiler_params=pltpu.CompilerParams(vmem_limit_bytes=8 * MIB),
        name="norm_pack",
    )(feats, ln_gain[None], ln_shift[None], cotangent)[None]
    parts = [held]
    step = 1
    while step < groups:
        held = parts[0] if len(parts) == 1 else jnp.concatenate(parts, axis=0)
        pairs = [(group, group ^ step) for group in range(groups)]
        parts = [held, lax.ppermute(held, "grp", pairs)]
        step *= 2
    column, grads = pl.pallas_call(
        functools.partial(unpack_kernel, block),
        out_shape=(
            jax.ShapeDtypeStruct((groups * block, vis_width), bfloat16),
            jax.ShapeDtypeStruct((all_rows, units), bfloat16),
        ),
        in_specs=[WHOLE] * len(parts),
        out_specs=(WHOLE, WHOLE),
        compiler_params=pltpu.CompilerParams(vmem_limit_bytes=8 * MIB),
        name="unpack",
    )(*parts)
    rows = lax.all_gather(column, "dev", axis=0, tiled=True)
    width = 256 if units % 256 == 0 else units
    projected, grad_bias, grad_pre, terms = pl.pallas_call(
        functools.partial(fused_kernel, block, own_rows, lanes, groups, width),
        out_shape=(
            jax.ShapeDtypeStruct((group_rows, units), bfloat16),
            jax.ShapeDtypeStruct((1, units), float32),
            jax.ShapeDtypeStruct((slot_count, units), bfloat16),
            jax.ShapeDtypeStruct((lanes * block, vis_width), bfloat16),
        ),
        in_specs=[SCALARS] * 4 + [WHOLE] * 3 + [LEFT],
        out_specs=(WHOLE,) * 4,
        scratch_shapes=[
            pltpu.VMEM((units // width, vis_width, width), bfloat16),
            pltpu.VMEM((lanes * block, vis_width), float32),
            pltpu.SemaphoreType.DMA((units // width,)),
        ],
        compiler_params=pltpu.CompilerParams(vmem_limit_bytes=24 * MIB),
        name="fused",
    )(my_group[None], img_seq, img_count, img_offset, rows, grads, b_proj[None], w_proj)
    swapped = lax.all_to_all(terms.reshape(lanes, block, vis_width), "dev", 0, 0)
    height = 128 if vis_width % 128 == 0 else vis_width
    grad_weight = pl.pallas_call(
        functools.partial(grad_weight_kernel, height),
        out_shape=jax.ShapeDtypeStruct((vis_width, units), float32),
        in_specs=[WHOLE] * 2,
        out_specs=LEFT,
        scratch_shapes=[
            pltpu.VMEM((vis_width, units), float32),
            pltpu.SemaphoreType.DMA((vis_width // height,)),
        ],
        compiler_params=pltpu.CompilerParams(vmem_limit_bytes=24 * MIB),
        cost_estimate=pl.CostEstimate(
            flops=2 * slot_count * vis_width * units, bytes_accessed=4 * vis_width * units, transcendentals=0
        ),
        name="grad_weight",
    )(rows, grad_pre)
    grad_normed = jnp.sum(swapped.astype(float32), axis=0)[:own_rows]
    unit_rows, inv_scale, _ = normalize(feats, ln_gain, ln_shift)
    grad_feats = backward_norm(grad_normed, ln_gain, unit_rows, inv_scale)
    return (projected, grad_feats, grad_weight, grad_bias[0])


def summed_plan(feats, ln_gain, ln_shift, w_proj, b_proj, cotangent, img_seq, img_count, img_offset):
    lane_count = lax.axis_size("dev")
    groups = lax.axis_size("grp")
    my_group = lax.axis_index("grp")
    own_rows = feats.shape[0]
    group_rows = own_rows * lane_count
    all_rows = group_rows * groups
    row_base = my_group * group_rows
    target = row_targets(img_seq, img_count, img_offset, all_rows, group_rows)
    source_rows = (
        jnp.zeros((all_rows,), jnp.int32).at[target].set(jnp.arange(all_rows, dtype=jnp.int32))
    )
    arrivals = lax.dynamic_slice_in_dim(source_rows, row_base, group_rows)
    whole = lax.all_gather(feats, "dev", axis=0, tiled=True)
    unit_rows, inv_scale, normed = normalize(whole, ln_gain, ln_shift)
    normed = normed.astype(jnp.bfloat16)
    pre_act = jnp.dot(normed, w_proj, preferred_element_type=jnp.float32) + b_proj
    acted, slope = gelu_and_slope(pre_act)
    local_cols = acted.astype(jnp.bfloat16)
    all_cols = lax.all_gather(local_cols, "grp", axis=0, tiled=True)
    projected = all_cols[arrivals]
    all_grads = lax.all_gather(cotangent, "grp", axis=0, tiled=True)
    own_targets = lax.dynamic_slice_in_dim(target, row_base, group_rows)
    upstream = all_grads[own_targets]
    grad_pre = (upstream.astype(jnp.float32) * slope).astype(jnp.bfloat16)
    weight_term = lax.dot_general(
        normed, grad_pre, (((0,), (0,)), ((), ())), preferred_element_type=jnp.float32
    )
    bias_term = jnp.sum(grad_pre.astype(jnp.float32), axis=0)
    vis_width = weight_term.shape[0]
    padded_rows = (vis_width + groups) // groups * groups
    joint_term = jnp.concatenate(
        [
            weight_term,
            bias_term[None, :],
            jnp.zeros((padded_rows - vis_width - 1, weight_term.shape[1]), jnp.float32),
        ],
        axis=0,
    )
    summed_share = lax.psum_scatter(joint_term, "grp", scatter_dimension=0, tiled=True)
    summed_whole = lax.all_gather(
        summed_share.astype(jnp.bfloat16), "grp", axis=0, tiled=True
    ).astype(summed_share.dtype)
    grad_weight = summed_whole[:vis_width]
    grad_bias = summed_whole[vis_width]
    grad_normed = lax.psum_scatter(
        lax.dot_general(
            grad_pre, w_proj, (((1,), (1,)), ((), ())), preferred_element_type=jnp.float32
        ),
        "dev",
        scatter_dimension=0,
        tiled=True,
    )
    lane_start = lax.axis_index("dev") * own_rows
    own_unit = lax.dynamic_slice_in_dim(unit_rows, lane_start, own_rows, 0)
    own_scale = lax.dynamic_slice_in_dim(inv_scale, lane_start, own_rows, 0)
    grad_feats = backward_norm(grad_normed, ln_gain, own_unit, own_scale)
    return (projected, grad_feats, grad_weight, grad_bias)


def local(*arrays):
    feats, w_proj = arrays[0], arrays[3]
    all_rows = feats.shape[0] * lax.axis_size("dev") * lax.axis_size("grp")
    groups = lax.axis_size("grp")
    lighter = all_rows * jnp.dtype(jnp.bfloat16).itemsize <= w_proj.shape[1] * jnp.dtype(jnp.float32).itemsize
    if lighter and groups & (groups - 1) == 0:
        return gathered_plan(*arrays)
    return summed_plan(*arrays)


def solution(mesh):
    placed = (
        P(("grp", "dev"), None),
        P(),
        P(),
        P(None, "dev"),
        P("dev"),
        P("grp", "dev"),
        P(),
        P(),
        P(),
    )
    return jax.shard_map(
        local,
        mesh=mesh,
        in_specs=placed,
        out_specs=(P("grp", "dev"), P(("grp", "dev"), None), P(None, "dev"), P("dev")),
        check_vma=False,
    )
```

```python
import functools

import jax
import jax.numpy as jnp
from jax import lax
from jax.experimental import pallas as pl
from jax.experimental.pallas import tpu as pltpu
from jax.sharding import PartitionSpec as P

epsilon = 1e-05
root_two_over_pi = 0.7978845608028654
cubic = 0.044715
MIB = 1 << 20
WHOLE = pl.BlockSpec(memory_space=pltpu.VMEM)
SCALARS = pl.BlockSpec(memory_space=pltpu.SMEM)
LEFT = pl.BlockSpec(memory_space=pl.ANY)


def row_targets(img_seq, img_count, img_offset, all_rows, seq_rows):
    image_ids = jnp.arange(img_count.shape[0], dtype=jnp.int32)
    img_starts = jnp.sum(
        jnp.where(image_ids[None, :] < image_ids[:, None], img_count[None, :], 0), axis=1
    )
    img_ends = img_starts + img_count
    row_ids = jnp.arange(all_rows, dtype=jnp.int32)
    member = (
        (row_ids[:, None] >= img_starts[None, :]) & (row_ids[:, None] < img_ends[None, :])
    ).astype(jnp.int32)
    base_rows = img_seq * seq_rows + img_offset - img_starts
    return jnp.sum(member * base_rows[None, :], axis=1) + row_ids


def normalize(rows, ln_gain, ln_shift):
    values = rows.astype(jnp.float32)
    row_mean = jnp.mean(values, axis=1, keepdims=True)
    centered = values - row_mean
    inv_scale = lax.rsqrt(jnp.mean(centered * centered, axis=1, keepdims=True) + epsilon)
    unit_rows = centered * inv_scale
    return (unit_rows, inv_scale, unit_rows * ln_gain + ln_shift)


def gelu_and_slope(values):
    square = values * values
    bent = jnp.tanh(root_two_over_pi * values * (1.0 + cubic * square))
    half = 0.5 * (1.0 + bent)
    slope = half + 0.5 * values * (1.0 - bent * bent) * (
        root_two_over_pi * (1.0 + 3.0 * cubic * square)
    )
    return values * half, slope


def backward_norm(grad_normed, ln_gain, unit_rows, inv_scale):
    scaled_grad = grad_normed * ln_gain
    grad_feats = inv_scale * (
        scaled_grad
        - jnp.mean(scaled_grad, axis=1, keepdims=True)
        - unit_rows * jnp.mean(scaled_grad * unit_rows, axis=1, keepdims=True)
    )
    return grad_feats.astype(jnp.bfloat16)


def norm_kernel(feats, gain, shift, cotangent, normed, grads):
    rows = normalize(feats[...], gain[...][None], shift[...][None])[2]
    empty = normed.shape[0] - rows.shape[0]
    if empty:
        rows = jnp.concatenate([rows, jnp.zeros((empty, rows.shape[1]), jnp.float32)], axis=0)
    normed[...] = rows.astype(jnp.bfloat16)
    grads[...] = cotangent[...]


def distance_of(place, groups):
    distance = jnp.zeros_like(place)
    step, bit = groups // 2, 1
    while step:
        distance = jnp.where((place & bit) != 0, distance + step, distance)
        step, bit = step // 2, bit * 2
    return distance


def slot_targets(my_group, block, own_rows, lanes, groups, img_seq, img_count, img_offset):
    group_rows = own_rows * lanes
    slots = lax.broadcasted_iota(jnp.int32, (1, lanes * groups * block), 1)
    within = slots & (block - 1)
    row_ids = (
        (my_group ^ distance_of((slots // block) & (groups - 1), groups)) * group_rows
        + slots // (block * groups) * own_rows
        + within
    )
    target = jnp.zeros_like(row_ids)
    start = jnp.int32(0)
    for image in range(img_seq.shape[0]):
        end = start + img_count[image]
        member = (row_ids >= start) & (row_ids < end)
        base = img_seq[image] * group_rows + img_offset[image] - start
        target = jnp.where(member, row_ids + base, target)
        start = end
    return jnp.where(within < own_rows, target, -1)


def fused_kernel(
    block, own_rows, lanes, groups, width,
    place, img_seq, img_count, img_offset, rows, grads, bias, w_far,
    projected, grad_bias, grad_pre, terms, w_near, total, arrived,
):
    units = w_far.shape[1]
    steps = units // width
    copies = [
        pltpu.make_async_copy(w_far.at[:, pl.ds(step * width, width)], w_near.at[step], arrived.at[step])
        for step in range(steps)
    ]
    for copy in copies:
        copy.start()
    group_rows = own_rows * lanes
    all_rows = group_rows * groups
    slot_count = lanes * groups * block
    my_group = place[0]
    target = slot_targets(my_group, block, own_rows, lanes, groups, img_seq, img_count, img_offset)
    places = lax.broadcasted_iota(jnp.int32, (all_rows, slot_count), 0)
    held = places // group_rows
    seq_rows = places - held * group_rows + (my_group ^ distance_of(held, groups)) * group_rows
    routes = (target == seq_rows).astype(jnp.float32)
    arrivals = routes[:group_rows].astype(jnp.bfloat16)
    sources = routes.T.astype(jnp.bfloat16)
    own_place = lax.broadcasted_iota(jnp.int32, (lanes * block, slot_count), 0)
    own_slot = lax.broadcasted_iota(jnp.int32, (lanes * block, slot_count), 1)
    keep = own_slot == own_place // block * (block * groups) + (own_place & (block - 1))
    keep = keep.astype(jnp.float32).astype(jnp.bfloat16)
    for step in range(steps):
        copies[step].wait()
        span = slice(step * width, (step + 1) * width)
        weights = w_near[step]
        pre_act = jnp.dot(rows[...], weights, preferred_element_type=jnp.float32) + bias[:, span]
        acted, slope = gelu_and_slope(pre_act)
        projected[:, span] = jnp.dot(
            arrivals, acted.astype(jnp.bfloat16), preferred_element_type=jnp.float32
        ).astype(jnp.bfloat16)
        upstream = jnp.dot(sources, grads[:, span], preferred_element_type=jnp.float32)
        pulled = (upstream * slope).astype(jnp.bfloat16)
        grad_pre[:, span] = pulled
        grad_bias[:, span] = jnp.sum(pulled.astype(jnp.float32), axis=0, keepdims=True)
        own = jnp.dot(keep, pulled, preferred_element_type=jnp.float32).astype(jnp.bfloat16)
        term = lax.dot_general(own, weights, (((1,), (1,)), ((), ())), preferred_element_type=jnp.float32)
        if step:
            term = total[...] + term
        if step + 1 < steps:
            total[...] = term
        else:
            terms[...] = term.astype(jnp.bfloat16)


def grad_weight_kernel(height, rows, grad_pre, far, near, left):
    copies = []
    for step in range(rows.shape[1] // height):
        span = slice(step * height, (step + 1) * height)
        near[span, :] = lax.dot_general(
            rows[:, span], grad_pre[...], (((0,), (0,)), ((), ())), preferred_element_type=jnp.float32
        )
        copies.append(pltpu.make_async_copy(near.at[span], far.at[span], left.at[step]))
        copies[-1].start()
    for copy in copies:
        copy.wait()


def in_hbm(*arrays):
    return [pltpu.with_memory_space_constraint(array, pltpu.HBM) for array in arrays]


def gathered_plan(feats, ln_gain, ln_shift, w_proj, b_proj, cotangent, img_seq, img_count, img_offset):
    lanes = lax.axis_size("dev")
    groups = lax.axis_size("grp")
    my_group = lax.axis_index("grp")
    own_rows, vis_width = feats.shape
    units = w_proj.shape[1]
    group_rows = own_rows * lanes
    all_rows = group_rows * groups
    block = pl.next_power_of_2(own_rows)
    slot_count = lanes * groups * block
    bfloat16, float32 = jnp.bfloat16, jnp.float32
    column, grads = pl.pallas_call(
        norm_kernel,
        out_shape=(
            jax.ShapeDtypeStruct((block, vis_width), bfloat16),
            jax.ShapeDtypeStruct(cotangent.shape, bfloat16),
        ),
        in_specs=[WHOLE] * 4,
        out_specs=(WHOLE, WHOLE),
        compiler_params=pltpu.CompilerParams(vmem_limit_bytes=8 * MIB),
        name="norm",
    )(*in_hbm(feats, ln_gain, ln_shift, cotangent))
    step = groups // 2
    while step:
        pairs = [(group, group ^ step) for group in range(groups)]
        column = jnp.concatenate([column, lax.ppermute(column, "grp", pairs)], axis=0)
        grads = jnp.concatenate([grads, lax.ppermute(grads, "grp", pairs)], axis=0)
        step //= 2
    rows = lax.all_gather(column, "dev", axis=0, tiled=True)
    width = 256 if units % 256 == 0 else units
    projected, grad_bias, grad_pre, terms = pl.pallas_call(
        functools.partial(fused_kernel, block, own_rows, lanes, groups, width),
        out_shape=(
            jax.ShapeDtypeStruct((group_rows, units), bfloat16),
            jax.ShapeDtypeStruct((1, units), float32),
            jax.ShapeDtypeStruct((slot_count, units), bfloat16),
            jax.ShapeDtypeStruct((lanes * block, vis_width), bfloat16),
        ),
        in_specs=[SCALARS] * 4 + [WHOLE] * 3 + [LEFT],
        out_specs=(WHOLE,) * 4,
        scratch_shapes=[
            pltpu.VMEM((units // width, vis_width, width), bfloat16),
            pltpu.VMEM((lanes * block, vis_width), float32),
            pltpu.SemaphoreType.DMA((units // width,)),
        ],
        compiler_params=pltpu.CompilerParams(vmem_limit_bytes=24 * MIB),
        name="fused",
    )(my_group[None], *in_hbm(img_seq, img_count, img_offset), rows, grads, *in_hbm(b_proj[None], w_proj))
    swapped = lax.all_to_all(terms.reshape(lanes, block, vis_width), "dev", 0, 0)
    height = 128 if vis_width % 128 == 0 else vis_width
    grad_weight = pl.pallas_call(
        functools.partial(grad_weight_kernel, height),
        out_shape=jax.ShapeDtypeStruct((vis_width, units), float32),
        in_specs=[WHOLE] * 2,
        out_specs=LEFT,
        scratch_shapes=[
            pltpu.VMEM((vis_width, units), float32),
            pltpu.SemaphoreType.DMA((vis_width // height,)),
        ],
        compiler_params=pltpu.CompilerParams(vmem_limit_bytes=24 * MIB),
        cost_estimate=pl.CostEstimate(
            flops=2 * slot_count * vis_width * units, bytes_accessed=4 * vis_width * units, transcendentals=0
        ),
        name="grad_weight",
    )(rows, grad_pre)
    grad_normed = jnp.sum(swapped.astype(float32), axis=0)[:own_rows]
    unit_rows, inv_scale, _ = normalize(feats, ln_gain, ln_shift)
    grad_feats = backward_norm(grad_normed, ln_gain, unit_rows, inv_scale)
    return (projected, grad_feats, grad_weight, grad_bias[0])


def summed_plan(feats, ln_gain, ln_shift, w_proj, b_proj, cotangent, img_seq, img_count, img_offset):
    lane_count = lax.axis_size("dev")
    groups = lax.axis_size("grp")
    my_group = lax.axis_index("grp")
    own_rows = feats.shape[0]
    group_rows = own_rows * lane_count
    all_rows = group_rows * groups
    row_base = my_group * group_rows
    target = row_targets(img_seq, img_count, img_offset, all_rows, group_rows)
    source_rows = (
        jnp.zeros((all_rows,), jnp.int32).at[target].set(jnp.arange(all_rows, dtype=jnp.int32))
    )
    arrivals = lax.dynamic_slice_in_dim(source_rows, row_base, group_rows)
    whole = lax.all_gather(feats, "dev", axis=0, tiled=True)
    unit_rows, inv_scale, normed = normalize(whole, ln_gain, ln_shift)
    normed = normed.astype(jnp.bfloat16)
    pre_act = jnp.dot(normed, w_proj, preferred_element_type=jnp.float32) + b_proj
    acted, slope = gelu_and_slope(pre_act)
    local_cols = acted.astype(jnp.bfloat16)
    all_cols = lax.all_gather(local_cols, "grp", axis=0, tiled=True)
    projected = all_cols[arrivals]
    all_grads = lax.all_gather(cotangent, "grp", axis=0, tiled=True)
    own_targets = lax.dynamic_slice_in_dim(target, row_base, group_rows)
    upstream = all_grads[own_targets]
    grad_pre = (upstream.astype(jnp.float32) * slope).astype(jnp.bfloat16)
    weight_term = lax.dot_general(
        normed, grad_pre, (((0,), (0,)), ((), ())), preferred_element_type=jnp.float32
    )
    bias_term = jnp.sum(grad_pre.astype(jnp.float32), axis=0)
    vis_width = weight_term.shape[0]
    padded_rows = (vis_width + groups) // groups * groups
    joint_term = jnp.concatenate(
        [
            weight_term,
            bias_term[None, :],
            jnp.zeros((padded_rows - vis_width - 1, weight_term.shape[1]), jnp.float32),
        ],
        axis=0,
    )
    summed_share = lax.psum_scatter(joint_term, "grp", scatter_dimension=0, tiled=True)
    summed_whole = lax.all_gather(
        summed_share.astype(jnp.bfloat16), "grp", axis=0, tiled=True
    ).astype(summed_share.dtype)
    grad_weight = summed_whole[:vis_width]
    grad_bias = summed_whole[vis_width]
    grad_normed = lax.psum_scatter(
        lax.dot_general(
            grad_pre, w_proj, (((1,), (1,)), ((), ())), preferred_element_type=jnp.float32
        ),
        "dev",
        scatter_dimension=0,
        tiled=True,
    )
    lane_start = lax.axis_index("dev") * own_rows
    own_unit = lax.dynamic_slice_in_dim(unit_rows, lane_start, own_rows, 0)
    own_scale = lax.dynamic_slice_in_dim(inv_scale, lane_start, own_rows, 0)
    grad_feats = backward_norm(grad_normed, ln_gain, own_unit, own_scale)
    return (projected, grad_feats, grad_weight, grad_bias)


def local(*arrays):
    feats, w_proj = arrays[0], arrays[3]
    all_rows = feats.shape[0] * lax.axis_size("dev") * lax.axis_size("grp")
    groups = lax.axis_size("grp")
    lighter = all_rows * jnp.dtype(jnp.bfloat16).itemsize <= w_proj.shape[1] * jnp.dtype(jnp.float32).itemsize
    if lighter and groups & (groups - 1) == 0:
        return gathered_plan(*arrays)
    return summed_plan(*arrays)


def solution(mesh):
    placed = (
        P(("grp", "dev"), None),
        P(),
        P(),
        P(None, "dev"),
        P("dev"),
        P("grp", "dev"),
        P(),
        P(),
        P(),
    )
    return jax.shard_map(
        local,
        mesh=mesh,
        in_specs=placed,
        out_specs=(P("grp", "dev"), P(("grp", "dev"), None), P(None, "dev"), P("dev")),
        check_vma=False,
    )
```

```python
import functools

import jax
import jax.numpy as jnp
from jax import lax
from jax.experimental import pallas as pl
from jax.experimental.pallas import tpu as pltpu
from jax.sharding import PartitionSpec as P

epsilon = 1e-05
root_two_over_pi = 0.7978845608028654
cubic = 0.044715
MIB = 1 << 20
WHOLE = pl.BlockSpec(memory_space=pltpu.VMEM)
SCALARS = pl.BlockSpec(memory_space=pltpu.SMEM)
LEFT = pl.BlockSpec(memory_space=pl.ANY)


def row_targets(img_seq, img_count, img_offset, all_rows, seq_rows):
    image_ids = jnp.arange(img_count.shape[0], dtype=jnp.int32)
    img_starts = jnp.sum(
        jnp.where(image_ids[None, :] < image_ids[:, None], img_count[None, :], 0), axis=1
    )
    img_ends = img_starts + img_count
    row_ids = jnp.arange(all_rows, dtype=jnp.int32)
    member = (
        (row_ids[:, None] >= img_starts[None, :]) & (row_ids[:, None] < img_ends[None, :])
    ).astype(jnp.int32)
    base_rows = img_seq * seq_rows + img_offset - img_starts
    return jnp.sum(member * base_rows[None, :], axis=1) + row_ids


def normalize(rows, ln_gain, ln_shift):
    values = rows.astype(jnp.float32)
    row_mean = jnp.mean(values, axis=1, keepdims=True)
    centered = values - row_mean
    inv_scale = lax.rsqrt(jnp.mean(centered * centered, axis=1, keepdims=True) + epsilon)
    unit_rows = centered * inv_scale
    return (unit_rows, inv_scale, unit_rows * ln_gain + ln_shift)


def gelu_and_slope(values):
    square = values * values
    bent = jnp.tanh(root_two_over_pi * values * (1.0 + cubic * square))
    half = 0.5 * (1.0 + bent)
    slope = half + 0.5 * values * (1.0 - bent * bent) * (
        root_two_over_pi * (1.0 + 3.0 * cubic * square)
    )
    return values * half, slope


def backward_norm(grad_normed, ln_gain, unit_rows, inv_scale):
    scaled_grad = grad_normed * ln_gain
    grad_feats = inv_scale * (
        scaled_grad
        - jnp.mean(scaled_grad, axis=1, keepdims=True)
        - unit_rows * jnp.mean(scaled_grad * unit_rows, axis=1, keepdims=True)
    )
    return grad_feats.astype(jnp.bfloat16)


def norm_kernel(feats, gain, shift, cotangent, normed, grads, unit, scale, gain_near):
    unit_rows, inv_scale, rows = normalize(feats[...], gain[...][None], shift[...][None])
    empty = normed.shape[0] - rows.shape[0]
    if empty:
        rows = jnp.concatenate([rows, jnp.zeros((empty, rows.shape[1]), jnp.float32)], axis=0)
    normed[...] = rows.astype(jnp.bfloat16)
    grads[...] = cotangent[...]
    unit[...] = unit_rows
    scale[...] = jnp.broadcast_to(inv_scale, scale.shape)
    gain_near[...] = gain[...][None]


def distance_of(place, groups):
    distance = jnp.zeros_like(place)
    step, bit = groups // 2, 1
    while step:
        distance = jnp.where((place & bit) != 0, distance + step, distance)
        step, bit = step // 2, bit * 2
    return distance


def slot_targets(my_group, block, own_rows, lanes, groups, img_seq, img_count, img_offset):
    group_rows = own_rows * lanes
    slots = lax.broadcasted_iota(jnp.int32, (1, lanes * groups * block), 1)
    within = slots & (block - 1)
    row_ids = (
        (my_group ^ distance_of((slots // block) & (groups - 1), groups)) * group_rows
        + slots // (block * groups) * own_rows
        + within
    )
    target = jnp.zeros_like(row_ids)
    start = jnp.int32(0)
    for image in range(img_seq.shape[0]):
        end = start + img_count[image]
        member = (row_ids >= start) & (row_ids < end)
        base = img_seq[image] * group_rows + img_offset[image] - start
        target = jnp.where(member, row_ids + base, target)
        start = end
    return jnp.where(within < own_rows, target, -1)


def fetch_kernel(first, w_far, after, near, arrived):
    del after
    copy = pltpu.make_async_copy(w_far.at[pl.ds(first, near.shape[0])], near, arrived)
    copy.start()
    copy.wait()


def fetch_and_route_kernel(
    first, block, own_rows, lanes, groups,
    place, img_seq, img_count, img_offset, bias_far, w_far, after,
    near, bias, sources, own_sources, arrivals, arrived,
):
    del after
    copy = pltpu.make_async_copy(w_far.at[pl.ds(first, near.shape[0])], near, arrived)
    copy.start()
    bias[...] = bias_far[...]
    group_rows = own_rows * lanes
    slot_count = lanes * groups * block
    my_group = place[0]
    target = slot_targets(my_group, block, own_rows, lanes, groups, img_seq, img_count, img_offset)
    places = lax.broadcasted_iota(jnp.int32, (group_rows * groups, slot_count), 0)
    held = places // group_rows
    seq_rows = places - held * group_rows + (my_group ^ distance_of(held, groups)) * group_rows
    routes = (target == seq_rows).astype(jnp.float32)
    arrivals[...] = routes[:group_rows].astype(jnp.bfloat16)
    turned = routes.T
    sources[...] = turned.astype(jnp.bfloat16)
    own_sources[...] = own_slots(turned, block, lanes, groups).astype(jnp.bfloat16)
    copy.wait()


def own_slots(rows, block, lanes, groups):
    stride = block * groups
    return jnp.concatenate([rows[lane * stride : lane * stride + block] for lane in range(lanes)], axis=0)


def terms_kernel(block, lanes, groups, rows, grads, bias, own_sources, *refs):
    parts, (pre_act, terms) = refs[:-2], refs[-2:]
    total, first = bias[...], 0
    for part in parts:
        total = total + jnp.dot(
            rows[:, first : first + part.shape[0]], part[...], preferred_element_type=jnp.float32
        )
        first += part.shape[0]
    pre_act[...] = total
    slope = gelu_and_slope(own_slots(total, block, lanes, groups))[1]
    upstream = jnp.dot(own_sources[...], grads[...], preferred_element_type=jnp.float32)
    own = (upstream * slope).astype(jnp.bfloat16)
    first = 0
    for part in parts:
        term = lax.dot_general(own, part[...], (((1,), (1,)), ((), ())), preferred_element_type=jnp.float32)
        for lane in range(lanes):
            terms[lane, :, first : first + part.shape[0]] = term[
                lane * block : (lane + 1) * block
            ].astype(jnp.bfloat16)
        first += part.shape[0]


def grad_weight_kernel(
    height, rows, grads, pre_act, sources, arrivals, projected, grad_bias, far, grad_pre, near, left
):
    acted, slope = gelu_and_slope(pre_act[...])
    upstream = jnp.dot(sources[...], grads[...], preferred_element_type=jnp.float32)
    pulled = (upstream * slope).astype(jnp.bfloat16)
    grad_pre[...] = pulled
    copies = []
    for step in range(rows.shape[1] // height):
        span = slice(step * height, (step + 1) * height)
        near[span, :] = lax.dot_general(
            rows[:, span], grad_pre[...], (((0,), (0,)), ((), ())), preferred_element_type=jnp.float32
        )
        copies.append(pltpu.make_async_copy(near.at[span], far.at[span], left.at[step]))
        copies[-1].start()
    projected[...] = jnp.dot(
        arrivals[...], acted.astype(jnp.bfloat16), preferred_element_type=jnp.float32
    ).astype(jnp.bfloat16)
    grad_bias[...] = jnp.sum(pulled.astype(jnp.float32), axis=0, keepdims=True)
    for copy in copies:
        copy.wait()


def finish_kernel(swapped, gain, unit, scale, grad_feats):
    total = swapped[0].astype(jnp.float32)
    for lane in range(1, swapped.shape[0]):
        total = total + swapped[lane].astype(jnp.float32)
    grad_feats[...] = backward_norm(total[: unit.shape[0]], gain[...], unit[...], scale[:, :1])


def in_hbm(*arrays):
    return [pltpu.with_memory_space_constraint(array, pltpu.HBM) for array in arrays]


def near_call(kernel, name, outs, in_specs, operands, scratch=(), out_specs=None, moved=0, limit=24):
    return pl.pallas_call(
        kernel,
        out_shape=outs,
        in_specs=in_specs,
        out_specs=out_specs or (WHOLE,) * len(outs),
        scratch_shapes=list(scratch),
        compiler_params=pltpu.CompilerParams(vmem_limit_bytes=limit * MIB),
        cost_estimate=pl.CostEstimate(flops=0, bytes_accessed=moved, transcendentals=0),
        name=name,
    )(*operands)


def gathered_plan(feats, ln_gain, ln_shift, w_proj, b_proj, cotangent, img_seq, img_count, img_offset):
    lanes = lax.axis_size("dev")
    groups = lax.axis_size("grp")
    my_group = lax.axis_index("grp")
    own_rows, vis_width = feats.shape
    units = w_proj.shape[1]
    group_rows = own_rows * lanes
    all_rows = group_rows * groups
    block = pl.next_power_of_2(own_rows)
    slot_count = lanes * groups * block
    half = vis_width // 256 * 128
    shape, bfloat16, float32 = jax.ShapeDtypeStruct, jnp.bfloat16, jnp.float32
    w_far, bias_far = in_hbm(w_proj, b_proj[None])

    def exchange(held, step):
        pairs = [(group, group ^ step) for group in range(groups)]
        return jnp.concatenate([held, lax.ppermute(held, "grp", pairs)], axis=0)

    column, grads, unit, scale, gain = near_call(
        norm_kernel,
        "norm",
        (
            shape((block, vis_width), bfloat16),
            shape(cotangent.shape, bfloat16),
            shape(feats.shape, float32),
            shape((own_rows, 128), float32),
            shape((1, vis_width), float32),
        ),
        [WHOLE] * 4,
        in_hbm(feats, ln_gain, ln_shift, cotangent),
        limit=8,
    )
    (w_low,) = near_call(
        functools.partial(fetch_kernel, 0),
        "fetch",
        (shape((half, units), bfloat16),),
        [LEFT, LEFT],
        (w_far, column),
        [pltpu.SemaphoreType.DMA],
        moved=2 * half * units,
    )
    step = groups // 2
    while step:
        column, grads = exchange(column, step), exchange(grads, step)
        if step == groups // 2:
            later = column
        step //= 2
    w_high, bias, sources, own_sources, arrivals = near_call(
        functools.partial(fetch_and_route_kernel, half, block, own_rows, lanes, groups),
        "fetch_and_route",
        (
            shape((vis_width - half, units), bfloat16),
            shape((1, units), float32),
            shape((slot_count, all_rows), bfloat16),
            shape((lanes * block, all_rows), bfloat16),
            shape((group_rows, slot_count), bfloat16),
        ),
        [SCALARS] * 4 + [WHOLE, LEFT, LEFT],
        (my_group[None], *in_hbm(img_seq, img_count, img_offset), bias_far, w_far, later),
        [pltpu.SemaphoreType.DMA],
        moved=2 * (vis_width - half) * units,
    )
    rows = lax.all_gather(column, "dev", axis=0, tiled=True)
    pre_act, terms = near_call(
        functools.partial(terms_kernel, block, lanes, groups),
        "terms",
        (shape((slot_count, units), float32), shape((lanes, block, vis_width), bfloat16)),
        [WHOLE] * 6,
        (rows, grads, bias, own_sources, w_low, w_high),
        moved=4 * vis_width * units,
    )
    swapped = lax.all_to_all(terms, "dev", 0, 0)
    height = 128 if vis_width % 128 == 0 else vis_width
    projected, grad_bias, grad_weight = near_call(
        functools.partial(grad_weight_kernel, height),
        "grad_weight",
        (
            shape((group_rows, units), bfloat16),
            shape((1, units), float32),
            shape((vis_width, units), float32),
        ),
        [WHOLE] * 5,
        (rows, grads, pre_act, sources, arrivals),
        [
            pltpu.VMEM((slot_count, units), bfloat16),
            pltpu.VMEM((vis_width, units), float32),
            pltpu.SemaphoreType.DMA((vis_width // height,)),
        ],
        (WHOLE, WHOLE, LEFT),
        moved=4 * vis_width * units,
    )
    (grad_feats,) = near_call(
        finish_kernel,
        "finish",
        (shape(feats.shape, bfloat16),),
        [WHOLE] * 4,
        (swapped, gain, unit, scale),
        limit=8,
    )
    return (projected, grad_feats, grad_weight, grad_bias[0])


def summed_plan(feats, ln_gain, ln_shift, w_proj, b_proj, cotangent, img_seq, img_count, img_offset):
    lane_count = lax.axis_size("dev")
    groups = lax.axis_size("grp")
    my_group = lax.axis_index("grp")
    own_rows = feats.shape[0]
    group_rows = own_rows * lane_count
    all_rows = group_rows * groups
    row_base = my_group * group_rows
    target = row_targets(img_seq, img_count, img_offset, all_rows, group_rows)
    source_rows = (
        jnp.zeros((all_rows,), jnp.int32).at[target].set(jnp.arange(all_rows, dtype=jnp.int32))
    )
    arrivals = lax.dynamic_slice_in_dim(source_rows, row_base, group_rows)
    whole = lax.all_gather(feats, "dev", axis=0, tiled=True)
    unit_rows, inv_scale, normed = normalize(whole, ln_gain, ln_shift)
    normed = normed.astype(jnp.bfloat16)
    pre_act = jnp.dot(normed, w_proj, preferred_element_type=jnp.float32) + b_proj
    acted, slope = gelu_and_slope(pre_act)
    local_cols = acted.astype(jnp.bfloat16)
    all_cols = lax.all_gather(local_cols, "grp", axis=0, tiled=True)
    projected = all_cols[arrivals]
    all_grads = lax.all_gather(cotangent, "grp", axis=0, tiled=True)
    own_targets = lax.dynamic_slice_in_dim(target, row_base, group_rows)
    upstream = all_grads[own_targets]
    grad_pre = (upstream.astype(jnp.float32) * slope).astype(jnp.bfloat16)
    weight_term = lax.dot_general(
        normed, grad_pre, (((0,), (0,)), ((), ())), preferred_element_type=jnp.float32
    )
    bias_term = jnp.sum(grad_pre.astype(jnp.float32), axis=0)
    vis_width = weight_term.shape[0]
    padded_rows = (vis_width + groups) // groups * groups
    joint_term = jnp.concatenate(
        [
            weight_term,
            bias_term[None, :],
            jnp.zeros((padded_rows - vis_width - 1, weight_term.shape[1]), jnp.float32),
        ],
        axis=0,
    )
    summed_share = lax.psum_scatter(joint_term, "grp", scatter_dimension=0, tiled=True)
    summed_whole = lax.all_gather(
        summed_share.astype(jnp.bfloat16), "grp", axis=0, tiled=True
    ).astype(summed_share.dtype)
    grad_weight = summed_whole[:vis_width]
    grad_bias = summed_whole[vis_width]
    grad_normed = lax.psum_scatter(
        lax.dot_general(
            grad_pre, w_proj, (((1,), (1,)), ((), ())), preferred_element_type=jnp.float32
        ),
        "dev",
        scatter_dimension=0,
        tiled=True,
    )
    lane_start = lax.axis_index("dev") * own_rows
    own_unit = lax.dynamic_slice_in_dim(unit_rows, lane_start, own_rows, 0)
    own_scale = lax.dynamic_slice_in_dim(inv_scale, lane_start, own_rows, 0)
    grad_feats = backward_norm(grad_normed, ln_gain, own_unit, own_scale)
    return (projected, grad_feats, grad_weight, grad_bias)


def local(*arrays):
    feats, w_proj = arrays[0], arrays[3]
    all_rows = feats.shape[0] * lax.axis_size("dev") * lax.axis_size("grp")
    groups = lax.axis_size("grp")
    lighter = all_rows * jnp.dtype(jnp.bfloat16).itemsize <= w_proj.shape[1] * jnp.dtype(jnp.float32).itemsize
    if lighter and groups & (groups - 1) == 0:
        return gathered_plan(*arrays)
    return summed_plan(*arrays)


def solution(mesh):
    placed = (
        P(("grp", "dev"), None),
        P(),
        P(),
        P(None, "dev"),
        P("dev"),
        P("grp", "dev"),
        P(),
        P(),
        P(),
    )
    return jax.shard_map(
        local,
        mesh=mesh,
        in_specs=placed,
        out_specs=(P("grp", "dev"), P(("grp", "dev"), None), P(None, "dev"), P("dev")),
        check_vma=False,
    )
```

```python
import functools

import jax
import jax.numpy as jnp
from jax import lax
from jax.experimental import pallas as pl
from jax.experimental.pallas import tpu as pltpu
from jax.sharding import PartitionSpec as P

epsilon = 1e-05
root_two_over_pi = 0.7978845608028654
cubic = 0.044715
MIB = 1 << 20
WHOLE = pl.BlockSpec(memory_space=pltpu.VMEM)
SCALARS = pl.BlockSpec(memory_space=pltpu.SMEM)
LEFT = pl.BlockSpec(memory_space=pl.ANY)


def row_targets(img_seq, img_count, img_offset, all_rows, seq_rows):
    image_ids = jnp.arange(img_count.shape[0], dtype=jnp.int32)
    img_starts = jnp.sum(
        jnp.where(image_ids[None, :] < image_ids[:, None], img_count[None, :], 0), axis=1
    )
    img_ends = img_starts + img_count
    row_ids = jnp.arange(all_rows, dtype=jnp.int32)
    member = (
        (row_ids[:, None] >= img_starts[None, :]) & (row_ids[:, None] < img_ends[None, :])
    ).astype(jnp.int32)
    base_rows = img_seq * seq_rows + img_offset - img_starts
    return jnp.sum(member * base_rows[None, :], axis=1) + row_ids


def normalize(rows, ln_gain, ln_shift):
    values = rows.astype(jnp.float32)
    row_mean = jnp.mean(values, axis=1, keepdims=True)
    centered = values - row_mean
    inv_scale = lax.rsqrt(jnp.mean(centered * centered, axis=1, keepdims=True) + epsilon)
    unit_rows = centered * inv_scale
    return (unit_rows, inv_scale, unit_rows * ln_gain + ln_shift)


def gelu_and_slope(values):
    square = values * values
    bent = jnp.tanh(root_two_over_pi * values * (1.0 + cubic * square))
    half = 0.5 * (1.0 + bent)
    slope = half + 0.5 * values * (1.0 - bent * bent) * (
        root_two_over_pi * (1.0 + 3.0 * cubic * square)
    )
    return values * half, slope


def backward_norm(grad_normed, ln_gain, unit_rows, inv_scale):
    scaled_grad = grad_normed * ln_gain
    grad_feats = inv_scale * (
        scaled_grad
        - jnp.mean(scaled_grad, axis=1, keepdims=True)
        - unit_rows * jnp.mean(scaled_grad * unit_rows, axis=1, keepdims=True)
    )
    return grad_feats.astype(jnp.bfloat16)


def norm_kernel(*refs):
    parts, gain, shift, (normed, unit, scale) = refs[:-5], refs[-5], refs[-4], refs[-3:]
    blocks = [part[at] for part in parts for at in range(part.shape[0])]
    block, own_rows = normed.shape[0] // len(blocks), unit.shape[0]
    rows = []
    for at, held in enumerate(blocks):
        unit_rows, inv_scale, made = normalize(held, gain[...], shift[...])
        rows.append(made)
        if block > own_rows:
            rows.append(jnp.zeros((block - own_rows, made.shape[1]), jnp.float32))
        if at == 0:
            unit[...] = unit_rows
            scale[...] = jnp.broadcast_to(inv_scale, scale.shape)
    normed[...] = jnp.concatenate(rows, axis=0).astype(jnp.bfloat16)


def distance_of(place, groups):
    distance = jnp.zeros_like(place)
    step, bit = groups // 2, 1
    while step:
        distance = jnp.where((place & bit) != 0, distance + step, distance)
        step, bit = step // 2, bit * 2
    return distance


def slot_targets(my_group, block, own_rows, lanes, groups, img_seq, img_count, img_offset):
    group_rows = own_rows * lanes
    slots = lax.broadcasted_iota(jnp.int32, (1, lanes * groups * block), 1)
    within = slots & (block - 1)
    row_ids = (
        (my_group ^ distance_of((slots // block) & (groups - 1), groups)) * group_rows
        + slots // (block * groups) * own_rows
        + within
    )
    target = jnp.zeros_like(row_ids)
    start = jnp.int32(0)
    for image in range(img_seq.shape[0]):
        end = start + img_count[image]
        member = (row_ids >= start) & (row_ids < end)
        base = img_seq[image] * group_rows + img_offset[image] - start
        target = jnp.where(member, row_ids + base, target)
        start = end
    return jnp.where(within < own_rows, target, -1)


def join_kernel(*refs):
    parts, out, first = refs[:-1], refs[-1], 0
    for part in parts:
        out[first : first + part.shape[0]] = part[...]
        first += part.shape[0]


def fetch(first, w_far, near, arrived):
    copy = pltpu.make_async_copy(w_far.at[pl.ds(first, near.shape[0])], near, arrived)
    copy.start()
    return copy


def load_all(pairs, small):
    loads = [pltpu.make_async_copy(far, close, small.at[at]) for at, (far, close) in enumerate(pairs)]
    for load in loads:
        load.start()
    return loads


def fetch_kernel(
    first, place, w_far, feats_far, grads_far, gain_far, shift_far,
    near, feats, grads, gain, shift, gain_line, shift_line, arrived, small,
):
    del place
    copy = fetch(first, w_far, near, arrived)
    pairs = ((feats_far, feats.at[0]), (grads_far, grads), (gain_far, gain_line), (shift_far, shift_line))
    for load in load_all(pairs, small):
        load.wait()
    gain[...] = gain_line[...][None]
    shift[...] = shift_line[...][None]
    copy.wait()


def fetch_and_route_kernel(
    first, block, own_rows, lanes, groups,
    place, img_seq_far, img_count_far, img_offset_far, bias_far, w_far, after,
    near, bias, sources, own_sources, arrivals,
    img_seq, img_count, img_offset, arrived, small,
):
    del after
    copy = fetch(first, w_far, near, arrived)
    pairs = (
        (img_seq_far, img_seq),
        (img_count_far, img_count),
        (img_offset_far, img_offset),
        (bias_far, bias),
    )
    for load in load_all(pairs, small):
        load.wait()
    group_rows = own_rows * lanes
    slot_count = lanes * groups * block
    my_group = place[0]
    target = slot_targets(my_group, block, own_rows, lanes, groups, img_seq, img_count, img_offset)
    places = lax.broadcasted_iota(jnp.int32, (group_rows * groups, slot_count), 0)
    held = places // group_rows
    seq_rows = places - held * group_rows + (my_group ^ distance_of(held, groups)) * group_rows
    routes = (target == seq_rows).astype(jnp.float32)
    arrivals[...] = routes[:group_rows].astype(jnp.bfloat16)
    turned = routes.T
    sources[...] = turned.astype(jnp.bfloat16)
    own_sources[...] = own_slots(turned, block, lanes, groups).astype(jnp.bfloat16)
    copy.wait()


def own_slots(rows, block, lanes, groups):
    stride = block * groups
    return jnp.concatenate([rows[lane * stride : lane * stride + block] for lane in range(lanes)], axis=0)


def terms_kernel(block, lanes, groups, width, rows, grads, bias, own_sources, *refs):
    parts, (pre_act, far, terms, left) = refs[:-4], refs[-4:]
    total, first = bias[...], 0
    for part in parts:
        total = total + jnp.dot(
            rows[:, first : first + part.shape[0]], part[...], preferred_element_type=jnp.float32
        )
        first += part.shape[0]
    pre_act[...] = total
    slope = gelu_and_slope(own_slots(total, block, lanes, groups))[1]
    upstream = jnp.dot(own_sources[...], grads[...], preferred_element_type=jnp.float32)
    own = (upstream * slope).astype(jnp.bfloat16)
    first, copies = 0, []
    for part in parts:
        for start in range(0, part.shape[0], width):
            size = min(width, part.shape[0] - start)
            term = lax.dot_general(
                own, part[start : start + size], (((1,), (1,)), ((), ())), preferred_element_type=jnp.float32
            )
            span = slice(first, first + size)
            for lane in range(lanes):
                terms[lane, :, span] = term[lane * block : (lane + 1) * block].astype(jnp.bfloat16)
            copies.append(
                pltpu.make_async_copy(terms.at[:, :, span], far.at[:, :, span], left.at[len(copies)])
            )
            copies[-1].start()
            first += size
    for copy in copies:
        copy.wait()


def grad_weight_kernel(
    height, rows, grads, pre_act, sources, arrivals, projected, grad_bias, far, grad_pre, near, left
):
    acted, slope = gelu_and_slope(pre_act[...])
    upstream = jnp.dot(sources[...], grads[...], preferred_element_type=jnp.float32)
    pulled = (upstream * slope).astype(jnp.bfloat16)
    grad_pre[...] = pulled
    copies = []
    for step in range(rows.shape[1] // height):
        span = slice(step * height, (step + 1) * height)
        near[span, :] = lax.dot_general(
            rows[:, span], grad_pre[...], (((0,), (0,)), ((), ())), preferred_element_type=jnp.float32
        )
        copies.append(pltpu.make_async_copy(near.at[span], far.at[span], left.at[step]))
        copies[-1].start()
    projected[...] = jnp.dot(
        arrivals[...], acted.astype(jnp.bfloat16), preferred_element_type=jnp.float32
    ).astype(jnp.bfloat16)
    grad_bias[...] = jnp.sum(pulled.astype(jnp.float32), axis=0, keepdims=True)
    for copy in copies:
        copy.wait()


def finish_kernel(swapped, gain, unit, scale, grad_feats):
    total = swapped[0].astype(jnp.float32)
    for lane in range(1, swapped.shape[0]):
        total = total + swapped[lane].astype(jnp.float32)
    grad_feats[...] = backward_norm(total[: unit.shape[0]], gain[...], unit[...], scale[:, :1])


def in_hbm(*arrays):
    return [pltpu.with_memory_space_constraint(array, pltpu.HBM) for array in arrays]


def near_call(kernel, name, outs, in_specs, operands, scratch=(), out_specs=None, moved=0, limit=24):
    return pl.pallas_call(
        kernel,
        out_shape=outs,
        in_specs=in_specs,
        out_specs=out_specs or (WHOLE,) * len(outs),
        scratch_shapes=list(scratch),
        compiler_params=pltpu.CompilerParams(vmem_limit_bytes=limit * MIB),
        cost_estimate=pl.CostEstimate(flops=0, bytes_accessed=moved, transcendentals=0),
        name=name,
    )(*operands)


def gathered_plan(feats, ln_gain, ln_shift, w_proj, b_proj, cotangent, img_seq, img_count, img_offset):
    lanes = lax.axis_size("dev")
    groups = lax.axis_size("grp")
    my_group = lax.axis_index("grp")
    own_rows, vis_width = feats.shape
    units = w_proj.shape[1]
    group_rows = own_rows * lanes
    all_rows = group_rows * groups
    block = pl.next_power_of_2(own_rows)
    slot_count = lanes * groups * block
    half = vis_width // 256 * 128
    width = 896
    shape, bfloat16, float32 = jax.ShapeDtypeStruct, jnp.bfloat16, jnp.float32
    place = my_group[None]
    feats_far, w_far, bias_far = in_hbm(feats, w_proj, b_proj[None])

    def swap(held, step):
        return lax.ppermute(held, "grp", [(group, group ^ step) for group in range(groups)])

    def join(*parts):
        rows = sum(part.shape[0] for part in parts)
        outs = (shape((rows, *parts[0].shape[1:]), bfloat16),)
        return near_call(join_kernel, "join", outs, [WHOLE] * len(parts), parts, limit=8)[0]

    step = groups // 2
    if step:
        feats_swapped, grads_swapped = swap(feats[None], step), swap(cotangent, step)
    w_low, column, grads, gain, shift = near_call(
        functools.partial(fetch_kernel, 0),
        "fetch",
        (
            shape((half, units), bfloat16),
            shape((1, own_rows, vis_width), bfloat16),
            shape(cotangent.shape, bfloat16),
            shape((1, vis_width), float32),
            shape((1, vis_width), float32),
        ),
        [LEFT] * 6,
        (place, w_far, feats_far, *in_hbm(cotangent, ln_gain, ln_shift)),
        [
            pltpu.VMEM((vis_width,), float32),
            pltpu.VMEM((vis_width,), float32),
            pltpu.SemaphoreType.DMA,
            pltpu.SemaphoreType.DMA((4,)),
        ],
        moved=vis_width * units,
        limit=8,
    )
    blocks, later = [column], column
    while step:
        blocks = [column, feats_swapped]
        grads = join(grads, grads_swapped)
        step //= 2
        if step:
            column = later = join(*blocks)
            feats_swapped, grads_swapped = swap(column, step), swap(grads, step)
    w_high, bias, sources, own_sources, arrivals = near_call(
        functools.partial(fetch_and_route_kernel, half, block, own_rows, lanes, groups),
        "fetch_and_route",
        (
            shape((vis_width - half, units), bfloat16),
            shape((1, units), float32),
            shape((slot_count, all_rows), bfloat16),
            shape((lanes * block, all_rows), bfloat16),
            shape((group_rows, slot_count), bfloat16),
        ),
        [SCALARS] + [LEFT] * 6,
        (place, *in_hbm(img_seq, img_count, img_offset), bias_far, w_far, later),
        [pltpu.SMEM(img_seq.shape, jnp.int32)] * 3
        + [pltpu.SemaphoreType.DMA, pltpu.SemaphoreType.DMA((4,))],
        moved=vis_width * units,
        limit=8,
    )
    column, unit, scale = near_call(
        norm_kernel,
        "norm",
        (
            shape((groups * block, vis_width), bfloat16),
            shape(feats.shape, float32),
            shape((own_rows, 128), float32),
        ),
        [WHOLE] * (len(blocks) + 2),
        (*blocks, gain, shift),
        limit=8,
    )
    rows = lax.all_gather(column, "dev", axis=0, tiled=True)
    pre_act, terms = near_call(
        functools.partial(terms_kernel, block, lanes, groups, width),
        "terms",
        (shape((slot_count, units), float32), shape((lanes, block, vis_width), bfloat16)),
        [WHOLE] * 6,
        (rows, grads, bias, own_sources, w_low, w_high),
        [
            pltpu.VMEM((lanes, block, vis_width), bfloat16),
            pltpu.SemaphoreType.DMA((pl.cdiv(half, width) + pl.cdiv(vis_width - half, width),)),
        ],
        (WHOLE, LEFT),
        moved=4 * vis_width * units,
    )
    swapped = lax.all_to_all(terms, "dev", 0, 0)
    height = 128 if vis_width % 128 == 0 else vis_width
    projected, grad_bias, grad_weight = near_call(
        functools.partial(grad_weight_kernel, height),
        "grad_weight",
        (
            shape((group_rows, units), bfloat16),
            shape((1, units), float32),
            shape((vis_width, units), float32),
        ),
        [WHOLE] * 5,
        (rows, grads, pre_act, sources, arrivals),
        [
            pltpu.VMEM((slot_count, units), bfloat16),
            pltpu.VMEM((vis_width, units), float32),
            pltpu.SemaphoreType.DMA((vis_width // height,)),
        ],
        (WHOLE, WHOLE, LEFT),
        moved=4 * vis_width * units,
        limit=20,
    )
    (grad_feats,) = near_call(
        finish_kernel,
        "finish",
        (shape(feats.shape, bfloat16),),
        [WHOLE] * 4,
        (swapped, gain, unit, scale),
        limit=8,
    )
    return (projected, grad_feats, grad_weight, grad_bias[0])


def summed_plan(feats, ln_gain, ln_shift, w_proj, b_proj, cotangent, img_seq, img_count, img_offset):
    lane_count = lax.axis_size("dev")
    groups = lax.axis_size("grp")
    my_group = lax.axis_index("grp")
    own_rows = feats.shape[0]
    group_rows = own_rows * lane_count
    all_rows = group_rows * groups
    row_base = my_group * group_rows
    target = row_targets(img_seq, img_count, img_offset, all_rows, group_rows)
    source_rows = (
        jnp.zeros((all_rows,), jnp.int32).at[target].set(jnp.arange(all_rows, dtype=jnp.int32))
    )
    arrivals = lax.dynamic_slice_in_dim(source_rows, row_base, group_rows)
    whole = lax.all_gather(feats, "dev", axis=0, tiled=True)
    unit_rows, inv_scale, normed = normalize(whole, ln_gain, ln_shift)
    normed = normed.astype(jnp.bfloat16)
    pre_act = jnp.dot(normed, w_proj, preferred_element_type=jnp.float32) + b_proj
    acted, slope = gelu_and_slope(pre_act)
    local_cols = acted.astype(jnp.bfloat16)
    all_cols = lax.all_gather(local_cols, "grp", axis=0, tiled=True)
    projected = all_cols[arrivals]
    all_grads = lax.all_gather(cotangent, "grp", axis=0, tiled=True)
    own_targets = lax.dynamic_slice_in_dim(target, row_base, group_rows)
    upstream = all_grads[own_targets]
    grad_pre = (upstream.astype(jnp.float32) * slope).astype(jnp.bfloat16)
    weight_term = lax.dot_general(
        normed, grad_pre, (((0,), (0,)), ((), ())), preferred_element_type=jnp.float32
    )
    bias_term = jnp.sum(grad_pre.astype(jnp.float32), axis=0)
    vis_width = weight_term.shape[0]
    padded_rows = (vis_width + groups) // groups * groups
    joint_term = jnp.concatenate(
        [
            weight_term,
            bias_term[None, :],
            jnp.zeros((padded_rows - vis_width - 1, weight_term.shape[1]), jnp.float32),
        ],
        axis=0,
    )
    summed_share = lax.psum_scatter(joint_term, "grp", scatter_dimension=0, tiled=True)
    summed_whole = lax.all_gather(
        summed_share.astype(jnp.bfloat16), "grp", axis=0, tiled=True
    ).astype(summed_share.dtype)
    grad_weight = summed_whole[:vis_width]
    grad_bias = summed_whole[vis_width]
    grad_normed = lax.psum_scatter(
        lax.dot_general(
            grad_pre, w_proj, (((1,), (1,)), ((), ())), preferred_element_type=jnp.float32
        ),
        "dev",
        scatter_dimension=0,
        tiled=True,
    )
    lane_start = lax.axis_index("dev") * own_rows
    own_unit = lax.dynamic_slice_in_dim(unit_rows, lane_start, own_rows, 0)
    own_scale = lax.dynamic_slice_in_dim(inv_scale, lane_start, own_rows, 0)
    grad_feats = backward_norm(grad_normed, ln_gain, own_unit, own_scale)
    return (projected, grad_feats, grad_weight, grad_bias)


def local(*arrays):
    feats, w_proj = arrays[0], arrays[3]
    all_rows = feats.shape[0] * lax.axis_size("dev") * lax.axis_size("grp")
    groups = lax.axis_size("grp")
    lighter = all_rows * jnp.dtype(jnp.bfloat16).itemsize <= w_proj.shape[1] * jnp.dtype(jnp.float32).itemsize
    if lighter and groups & (groups - 1) == 0:
        return gathered_plan(*arrays)
    return summed_plan(*arrays)


def solution(mesh):
    placed = (
        P(("grp", "dev"), None),
        P(),
        P(),
        P(None, "dev"),
        P("dev"),
        P("grp", "dev"),
        P(),
        P(),
        P(),
    )
    return jax.shard_map(
        local,
        mesh=mesh,
        in_specs=placed,
        out_specs=(P("grp", "dev"), P(("grp", "dev"), None), P(None, "dev"), P("dev")),
        check_vma=False,
    )
```

```python
import functools

import jax
import jax.numpy as jnp
from jax import lax
from jax.experimental import pallas as pl
from jax.experimental.pallas import tpu as pltpu
from jax.sharding import PartitionSpec as P

epsilon = 1e-05
root_two_over_pi = 0.7978845608028654
cubic = 0.044715
MIB = 1 << 20
WHOLE = pl.BlockSpec(memory_space=pltpu.VMEM)
SCALARS = pl.BlockSpec(memory_space=pltpu.SMEM)
LEFT = pl.BlockSpec(memory_space=pl.ANY)


def row_targets(img_seq, img_count, img_offset, all_rows, seq_rows):
    image_ids = jnp.arange(img_count.shape[0], dtype=jnp.int32)
    img_starts = jnp.sum(
        jnp.where(image_ids[None, :] < image_ids[:, None], img_count[None, :], 0), axis=1
    )
    img_ends = img_starts + img_count
    row_ids = jnp.arange(all_rows, dtype=jnp.int32)
    member = (
        (row_ids[:, None] >= img_starts[None, :]) & (row_ids[:, None] < img_ends[None, :])
    ).astype(jnp.int32)
    base_rows = img_seq * seq_rows + img_offset - img_starts
    return jnp.sum(member * base_rows[None, :], axis=1) + row_ids


def normalize(rows, ln_gain, ln_shift):
    values = rows.astype(jnp.float32)
    row_mean = jnp.mean(values, axis=1, keepdims=True)
    centered = values - row_mean
    inv_scale = lax.rsqrt(jnp.mean(centered * centered, axis=1, keepdims=True) + epsilon)
    unit_rows = centered * inv_scale
    return (unit_rows, inv_scale, unit_rows * ln_gain + ln_shift)


def gelu_and_slope(values):
    square = values * values
    bent = jnp.tanh(root_two_over_pi * values * (1.0 + cubic * square))
    half = 0.5 * (1.0 + bent)
    slope = half + 0.5 * values * (1.0 - bent * bent) * (
        root_two_over_pi * (1.0 + 3.0 * cubic * square)
    )
    return values * half, slope


def backward_norm(grad_normed, ln_gain, unit_rows, inv_scale):
    scaled_grad = grad_normed * ln_gain
    grad_feats = inv_scale * (
        scaled_grad
        - jnp.mean(scaled_grad, axis=1, keepdims=True)
        - unit_rows * jnp.mean(scaled_grad * unit_rows, axis=1, keepdims=True)
    )
    return grad_feats.astype(jnp.bfloat16)


def norm_kernel(*refs):
    parts, gain, shift, (normed, unit, scale) = refs[:-5], refs[-5], refs[-4], refs[-3:]
    blocks = [part[at] for part in parts for at in range(part.shape[0])]
    rows = []
    for at, held in enumerate(blocks):
        unit_rows, inv_scale, made = normalize(held, gain[...], shift[...])
        rows.append(made)
        if at == 0:
            unit[...] = unit_rows
            scale[...] = jnp.broadcast_to(inv_scale, scale.shape)
    rows = jnp.concatenate(rows, axis=0)
    width = normed.shape[1]
    rest = fill(rows[:, width:], width)
    normed[...] = jnp.concatenate([rows[:, :width], rest], axis=0).astype(jnp.bfloat16)


def fill(rows, width):
    empty = width - rows.shape[1]
    if not empty:
        return rows
    return jnp.concatenate([rows, jnp.zeros((rows.shape[0], empty), rows.dtype)], axis=1)


def fold_width(own_rows, vis_width):
    lines = pl.cdiv(own_rows, 8) * 8
    width = pl.cdiv(own_rows * vis_width, lines * 128) * 128
    while True:
        rest = vis_width % width
        used = own_rows * (vis_width // width) + (pl.cdiv(own_rows, width // rest) if rest else 0)
        if used <= lines:
            return lines, width
        width += 128


def pack(rows, lines, width):
    own_rows, vis_width = rows.shape
    whole = vis_width // width * width
    parts = [rows[:, first : first + width] for first in range(0, whole, width)]
    if vis_width > whole:
        beside = width // (vis_width - whole)
        for first in range(0, own_rows, beside):
            last = min(first + beside, own_rows)
            line = jnp.concatenate([rows[row : row + 1, whole:] for row in range(first, last)], axis=1)
            parts.append(fill(line, width))
    empty = lines - sum(part.shape[0] for part in parts)
    if empty:
        parts.append(jnp.zeros((empty, width), rows.dtype))
    return jnp.concatenate(parts, axis=0)


def unpack(packed, own_rows, vis_width):
    width = packed.shape[1]
    count = vis_width // width
    rest = vis_width - count * width
    parts = [packed[at * own_rows : (at + 1) * own_rows] for at in range(count)]
    if rest:
        beside, base = width // rest, count * own_rows
        parts.append(
            jnp.concatenate(
                [
                    packed[base + row // beside : base + row // beside + 1, row % beside * rest : (row % beside + 1) * rest]
                    for row in range(own_rows)
                ],
                axis=0,
            )
        )
    return jnp.concatenate(parts, axis=1)


def distance_of(place, groups):
    distance = jnp.zeros_like(place)
    step, bit = groups // 2, 1
    while step:
        distance = jnp.where((place & bit) != 0, distance + step, distance)
        step, bit = step // 2, bit * 2
    return distance


def slot_targets(my_group, own_rows, lanes, groups, img_seq, img_count, img_offset):
    group_rows = own_rows * lanes
    slots = lax.broadcasted_iota(jnp.int32, (1, group_rows * groups), 1)
    lane = slots // (own_rows * groups)
    left = slots - lane * (own_rows * groups)
    held = left // own_rows
    row_ids = (my_group ^ distance_of(held, groups)) * group_rows + (lane - held) * own_rows + left
    target = jnp.zeros_like(row_ids)
    start = jnp.int32(0)
    for image in range(img_seq.shape[0]):
        end = start + img_count[image]
        member = (row_ids >= start) & (row_ids < end)
        base = img_seq[image] * group_rows + img_offset[image] - start
        target = jnp.where(member, row_ids + base, target)
        start = end
    return target


def join_kernel(*refs):
    parts, out, first = refs[:-1], refs[-1], 0
    for part in parts:
        out[first : first + part.shape[0]] = part[...]
        first += part.shape[0]


def fetch(first, w_far, near, arrived):
    copy = pltpu.make_async_copy(w_far.at[pl.ds(first, near.shape[0])], near, arrived)
    copy.start()
    return copy


def load_all(pairs, small):
    loads = [pltpu.make_async_copy(far, close, small.at[at]) for at, (far, close) in enumerate(pairs)]
    for load in loads:
        load.start()
    return loads


def fetch_kernel(
    first, place, w_far, feats_far, grads_far, gain_far, shift_far,
    near, feats, grads, gain, shift, gain_line, shift_line, arrived, small,
):
    del place
    copy = fetch(first, w_far, near, arrived)
    pairs = ((feats_far, feats.at[0]), (grads_far, grads), (gain_far, gain_line), (shift_far, shift_line))
    for load in load_all(pairs, small):
        load.wait()
    gain[...] = gain_line[...][None]
    shift[...] = shift_line[...][None]
    copy.wait()


def fetch_and_route_kernel(
    first, own_rows, lanes, groups,
    place, img_seq_far, img_count_far, img_offset_far, bias_far, w_far, after,
    near, bias, sources, own_sources, arrivals,
    img_seq, img_count, img_offset, arrived, small,
):
    del after
    copy = fetch(first, w_far, near, arrived)
    pairs = (
        (img_seq_far, img_seq),
        (img_count_far, img_count),
        (img_offset_far, img_offset),
        (bias_far, bias),
    )
    for load in load_all(pairs, small):
        load.wait()
    group_rows = own_rows * lanes
    all_rows = group_rows * groups
    my_group = place[0]
    target = slot_targets(my_group, own_rows, lanes, groups, img_seq, img_count, img_offset)
    places = lax.broadcasted_iota(jnp.int32, (all_rows, all_rows), 0)
    held = places // group_rows
    seq_rows = places - held * group_rows + (my_group ^ distance_of(held, groups)) * group_rows
    routes = (target == seq_rows).astype(jnp.float32)
    arrivals[...] = routes[:group_rows].astype(jnp.bfloat16)
    turned = routes.T
    sources[...] = turned.astype(jnp.bfloat16)
    own_sources[...] = own_slots(turned, own_rows, lanes, groups).astype(jnp.bfloat16)
    copy.wait()


def own_slots(rows, own_rows, lanes, groups):
    stride = own_rows * groups
    return jnp.concatenate([rows[lane * stride : lane * stride + own_rows] for lane in range(lanes)], axis=0)


def terms_kernel(
    own_rows, lanes, groups, packed, grads, bias, own_sources, low, high, rows, pre_act, far, terms, left
):
    stride = own_rows * groups
    held = packed[...].astype(jnp.float32)
    upper = [held[2 * lane * stride : (2 * lane + 1) * stride] for lane in range(lanes)]
    lower = [held[(2 * lane + 1) * stride : 2 * (lane + 1) * stride, : high.shape[0]] for lane in range(lanes)]
    upper = jnp.concatenate(upper, axis=0).astype(jnp.bfloat16)
    lower = jnp.concatenate(lower, axis=0).astype(jnp.bfloat16)
    rows[:, : low.shape[0]] = upper
    rows[:, low.shape[0] :] = lower
    total = bias[...] + jnp.dot(upper, low[...], preferred_element_type=jnp.float32)
    total = total + jnp.dot(lower, high[...], preferred_element_type=jnp.float32)
    pre_act[...] = total
    slope = gelu_and_slope(own_slots(total, own_rows, lanes, groups))[1]
    upstream = jnp.dot(own_sources[...], grads[...], preferred_element_type=jnp.float32)
    own = (upstream * slope).astype(jnp.bfloat16)
    term = jnp.concatenate(
        [
            lax.dot_general(own, part[...], (((1,), (1,)), ((), ())), preferred_element_type=jnp.float32)
            for part in (low, high)
        ],
        axis=1,
    )
    copies = []
    for lane in range(lanes):
        mine = term[lane * own_rows : (lane + 1) * own_rows]
        terms[lane] = pack(mine, terms.shape[1], terms.shape[2]).astype(jnp.bfloat16)
        copies.append(pltpu.make_async_copy(terms.at[lane], far.at[lane], left.at[lane]))
        copies[-1].start()
    for copy in copies:
        copy.wait()


def grad_weight_kernel(
    height, rows, grads, pre_act, sources, arrivals, projected_far, bias_far, far,
    projected, grad_bias, grad_pre, near, left, small,
):
    acted, slope = gelu_and_slope(pre_act[...])
    upstream = jnp.dot(sources[...], grads[...], preferred_element_type=jnp.float32)
    pulled = (upstream * slope).astype(jnp.bfloat16)
    grad_pre[...] = pulled
    copies = []
    for step in range(rows.shape[1] // height):
        span = slice(step * height, (step + 1) * height)
        near[span, :] = lax.dot_general(
            rows[:, span], grad_pre[...], (((0,), (0,)), ((), ())), preferred_element_type=jnp.float32
        )
        copies.append(pltpu.make_async_copy(near.at[span], far.at[span], left.at[step]))
        copies[-1].start()
        if step == 0:
            projected[...] = jnp.dot(
                arrivals[...], acted.astype(jnp.bfloat16), preferred_element_type=jnp.float32
            ).astype(jnp.bfloat16)
            grad_bias[...] = jnp.sum(pulled.astype(jnp.float32), axis=0, keepdims=True)
            for at, (close, out) in enumerate(((projected, projected_far), (grad_bias, bias_far))):
                copies.append(pltpu.make_async_copy(close, out, small.at[at]))
                copies[-1].start()
    for copy in copies:
        copy.wait()


def finish_kernel(swapped, gain, unit, scale, grad_feats):
    total = swapped[0].astype(jnp.float32)
    for lane in range(1, swapped.shape[0]):
        total = total + swapped[lane].astype(jnp.float32)
    grad_feats[...] = backward_norm(unpack(total, *unit.shape), gain[...], unit[...], scale[:, :1])


def in_hbm(*arrays):
    return [pltpu.with_memory_space_constraint(array, pltpu.HBM) for array in arrays]


def near_call(kernel, name, outs, in_specs, operands, scratch=(), out_specs=None, moved=0, limit=24):
    return pl.pallas_call(
        kernel,
        out_shape=outs,
        in_specs=in_specs,
        out_specs=out_specs or (WHOLE,) * len(outs),
        scratch_shapes=list(scratch),
        compiler_params=pltpu.CompilerParams(vmem_limit_bytes=limit * MIB),
        cost_estimate=pl.CostEstimate(flops=0, bytes_accessed=moved, transcendentals=0),
        name=name,
    )(*operands)


def gathered_plan(feats, ln_gain, ln_shift, w_proj, b_proj, cotangent, img_seq, img_count, img_offset):
    lanes = lax.axis_size("dev")
    groups = lax.axis_size("grp")
    my_group = lax.axis_index("grp")
    own_rows, vis_width = feats.shape
    units = w_proj.shape[1]
    group_rows = own_rows * lanes
    all_rows = group_rows * groups
    half = pl.cdiv(vis_width, 256) * 128
    lines, width = fold_width(own_rows, vis_width)
    shape, bfloat16, float32 = jax.ShapeDtypeStruct, jnp.bfloat16, jnp.float32
    place = my_group[None]
    feats_far, w_far, bias_far = in_hbm(feats, w_proj, b_proj[None])

    def swap(held, step):
        return lax.ppermute(held, "grp", [(group, group ^ step) for group in range(groups)])

    def join(*parts):
        rows = sum(part.shape[0] for part in parts)
        outs = (shape((rows, *parts[0].shape[1:]), bfloat16),)
        return near_call(join_kernel, "join", outs, [WHOLE] * len(parts), parts, limit=8)[0]

    step = groups // 2
    if step:
        feats_swapped, grads_swapped = swap(feats[None], step), swap(cotangent, step)
    w_low, column, grads, gain, shift = near_call(
        functools.partial(fetch_kernel, 0),
        "fetch",
        (
            shape((half, units), bfloat16),
            shape((1, own_rows, vis_width), bfloat16),
            shape(cotangent.shape, bfloat16),
            shape((1, vis_width), float32),
            shape((1, vis_width), float32),
        ),
        [LEFT] * 6,
        (place, w_far, feats_far, *in_hbm(cotangent, ln_gain, ln_shift)),
        [
            pltpu.VMEM((vis_width,), float32),
            pltpu.VMEM((vis_width,), float32),
            pltpu.SemaphoreType.DMA,
            pltpu.SemaphoreType.DMA((4,)),
        ],
        moved=vis_width * units,
        limit=8,
    )
    blocks, later = [column], column
    while step:
        blocks = [column, feats_swapped]
        grads = join(grads, grads_swapped)
        step //= 2
        if step:
            column = later = join(*blocks)
            feats_swapped, grads_swapped = swap(column, step), swap(grads, step)
    w_high, bias, sources, own_sources, arrivals = near_call(
        functools.partial(fetch_and_route_kernel, half, own_rows, lanes, groups),
        "fetch_and_route",
        (
            shape((vis_width - half, units), bfloat16),
            shape((1, units), float32),
            shape((all_rows, all_rows), bfloat16),
            shape((group_rows, all_rows), bfloat16),
            shape((group_rows, all_rows), bfloat16),
        ),
        [SCALARS] + [LEFT] * 6,
        (place, *in_hbm(img_seq, img_count, img_offset), bias_far, w_far, later),
        [pltpu.SMEM(img_seq.shape, jnp.int32)] * 3
        + [pltpu.SemaphoreType.DMA, pltpu.SemaphoreType.DMA((4,))],
        moved=vis_width * units,
        limit=8,
    )
    column, unit, scale = near_call(
        norm_kernel,
        "norm",
        (
            shape((2 * groups * own_rows, half), bfloat16),
            shape(feats.shape, float32),
            shape((own_rows, 128), float32),
        ),
        [WHOLE] * (len(blocks) + 2),
        (*blocks, gain, shift),
        limit=8,
    )
    packed = lax.all_gather(column, "dev", axis=0, tiled=True)
    rows, pre_act, terms = near_call(
        functools.partial(terms_kernel, own_rows, lanes, groups),
        "terms",
        (
            shape((all_rows, vis_width), bfloat16),
            shape((all_rows, units), float32),
            pltpu.HBM((lanes, lines, width), bfloat16),
        ),
        [WHOLE] * 6,
        (packed, grads, bias, own_sources, w_low, w_high),
        [pltpu.VMEM((lanes, lines, width), bfloat16), pltpu.SemaphoreType.DMA((lanes,))],
        (WHOLE, WHOLE, LEFT),
        moved=4 * vis_width * units,
    )
    swapped = lax.all_to_all(terms, "dev", 0, 0)
    height = 128 if vis_width % 128 == 0 else vis_width
    projected, grad_bias, grad_weight = near_call(
        functools.partial(grad_weight_kernel, height),
        "grad_weight",
        (
            pltpu.HBM((group_rows, units), bfloat16),
            pltpu.HBM((1, units), float32),
            pltpu.HBM((vis_width, units), float32),
        ),
        [WHOLE] * 5,
        (rows, grads, pre_act, sources, arrivals),
        [
            pltpu.VMEM((group_rows, units), bfloat16),
            pltpu.VMEM((1, units), float32),
            pltpu.VMEM((all_rows, units), bfloat16),
            pltpu.VMEM((vis_width, units), float32),
            pltpu.SemaphoreType.DMA((vis_width // height,)),
            pltpu.SemaphoreType.DMA((2,)),
        ],
        (LEFT,) * 3,
        moved=4 * vis_width * units,
        limit=20,
    )
    (grad_feats,) = near_call(
        finish_kernel,
        "finish",
        (shape(feats.shape, bfloat16),),
        [WHOLE] * 4,
        (swapped, gain, unit, scale),
        limit=8,
    )
    return (projected, grad_feats, grad_weight, grad_bias[0])


def summed_plan(feats, ln_gain, ln_shift, w_proj, b_proj, cotangent, img_seq, img_count, img_offset):
    lane_count = lax.axis_size("dev")
    groups = lax.axis_size("grp")
    my_group = lax.axis_index("grp")
    own_rows = feats.shape[0]
    group_rows = own_rows * lane_count
    all_rows = group_rows * groups
    row_base = my_group * group_rows
    target = row_targets(img_seq, img_count, img_offset, all_rows, group_rows)
    source_rows = (
        jnp.zeros((all_rows,), jnp.int32).at[target].set(jnp.arange(all_rows, dtype=jnp.int32))
    )
    arrivals = lax.dynamic_slice_in_dim(source_rows, row_base, group_rows)
    whole = lax.all_gather(feats, "dev", axis=0, tiled=True)
    unit_rows, inv_scale, normed = normalize(whole, ln_gain, ln_shift)
    normed = normed.astype(jnp.bfloat16)
    pre_act = jnp.dot(normed, w_proj, preferred_element_type=jnp.float32) + b_proj
    acted, slope = gelu_and_slope(pre_act)
    local_cols = acted.astype(jnp.bfloat16)
    all_cols = lax.all_gather(local_cols, "grp", axis=0, tiled=True)
    projected = all_cols[arrivals]
    all_grads = lax.all_gather(cotangent, "grp", axis=0, tiled=True)
    own_targets = lax.dynamic_slice_in_dim(target, row_base, group_rows)
    upstream = all_grads[own_targets]
    grad_pre = (upstream.astype(jnp.float32) * slope).astype(jnp.bfloat16)
    weight_term = lax.dot_general(
        normed, grad_pre, (((0,), (0,)), ((), ())), preferred_element_type=jnp.float32
    )
    bias_term = jnp.sum(grad_pre.astype(jnp.float32), axis=0)
    vis_width = weight_term.shape[0]
    padded_rows = (vis_width + groups) // groups * groups
    joint_term = jnp.concatenate(
        [
            weight_term,
            bias_term[None, :],
            jnp.zeros((padded_rows - vis_width - 1, weight_term.shape[1]), jnp.float32),
        ],
        axis=0,
    )
    summed_share = lax.psum_scatter(joint_term, "grp", scatter_dimension=0, tiled=True)
    summed_whole = lax.all_gather(
        summed_share.astype(jnp.bfloat16), "grp", axis=0, tiled=True
    ).astype(summed_share.dtype)
    grad_weight = summed_whole[:vis_width]
    grad_bias = summed_whole[vis_width]
    grad_normed = lax.psum_scatter(
        lax.dot_general(
            grad_pre, w_proj, (((1,), (1,)), ((), ())), preferred_element_type=jnp.float32
        ),
        "dev",
        scatter_dimension=0,
        tiled=True,
    )
    lane_start = lax.axis_index("dev") * own_rows
    own_unit = lax.dynamic_slice_in_dim(unit_rows, lane_start, own_rows, 0)
    own_scale = lax.dynamic_slice_in_dim(inv_scale, lane_start, own_rows, 0)
    grad_feats = backward_norm(grad_normed, ln_gain, own_unit, own_scale)
    return (projected, grad_feats, grad_weight, grad_bias)


def local(*arrays):
    feats, w_proj = arrays[0], arrays[3]
    all_rows = feats.shape[0] * lax.axis_size("dev") * lax.axis_size("grp")
    groups = lax.axis_size("grp")
    lighter = all_rows * jnp.dtype(jnp.bfloat16).itemsize <= w_proj.shape[1] * jnp.dtype(jnp.float32).itemsize
    if lighter and groups & (groups - 1) == 0:
        return gathered_plan(*arrays)
    return summed_plan(*arrays)


def solution(mesh):
    placed = (
        P(("grp", "dev"), None),
        P(),
        P(),
        P(None, "dev"),
        P("dev"),
        P("grp", "dev"),
        P(),
        P(),
        P(),
    )
    return jax.shard_map(
        local,
        mesh=mesh,
        in_specs=placed,
        out_specs=(P("grp", "dev"), P(("grp", "dev"), None), P(None, "dev"), P("dev")),
        check_vma=False,
    )
```

```python
import functools

import jax
import jax.numpy as jnp
from jax import lax
from jax.experimental import pallas as pl
from jax.experimental.pallas import tpu as pltpu
from jax.sharding import PartitionSpec as P

epsilon = 1e-05
root_two_over_pi = 0.7978845608028654
cubic = 0.044715
MIB = 1 << 20
WHOLE = pl.BlockSpec(memory_space=pltpu.VMEM)
SCALARS = pl.BlockSpec(memory_space=pltpu.SMEM)
LEFT = pl.BlockSpec(memory_space=pl.ANY)


def row_targets(img_seq, img_count, img_offset, all_rows, seq_rows):
    image_ids = jnp.arange(img_count.shape[0], dtype=jnp.int32)
    img_starts = jnp.sum(
        jnp.where(image_ids[None, :] < image_ids[:, None], img_count[None, :], 0), axis=1
    )
    img_ends = img_starts + img_count
    row_ids = jnp.arange(all_rows, dtype=jnp.int32)
    member = (
        (row_ids[:, None] >= img_starts[None, :]) & (row_ids[:, None] < img_ends[None, :])
    ).astype(jnp.int32)
    base_rows = img_seq * seq_rows + img_offset - img_starts
    return jnp.sum(member * base_rows[None, :], axis=1) + row_ids


def normalize(rows, ln_gain, ln_shift):
    values = rows.astype(jnp.float32)
    row_mean = jnp.mean(values, axis=1, keepdims=True)
    centered = values - row_mean
    inv_scale = lax.rsqrt(jnp.mean(centered * centered, axis=1, keepdims=True) + epsilon)
    unit_rows = centered * inv_scale
    return (unit_rows, inv_scale, unit_rows * ln_gain + ln_shift)


def gelu_and_slope(values):
    square = values * values
    bent = jnp.tanh(root_two_over_pi * values * (1.0 + cubic * square))
    half = 0.5 * (1.0 + bent)
    slope = half + 0.5 * values * (1.0 - bent * bent) * (
        root_two_over_pi * (1.0 + 3.0 * cubic * square)
    )
    return values * half, slope


def backward_norm(grad_normed, ln_gain, unit_rows, inv_scale):
    scaled_grad = grad_normed * ln_gain
    grad_feats = inv_scale * (
        scaled_grad
        - jnp.mean(scaled_grad, axis=1, keepdims=True)
        - unit_rows * jnp.mean(scaled_grad * unit_rows, axis=1, keepdims=True)
    )
    return grad_feats.astype(jnp.bfloat16)


def norm_kernel(*refs):
    parts, gain, shift, (normed, unit, scale) = refs[:-5], refs[-5], refs[-4], refs[-3:]
    blocks = [part[at].astype(jnp.float32) for part in parts for at in range(part.shape[0])]
    unit_rows, inv_scale, rows = normalize(jnp.concatenate(blocks, axis=0), gain[...], shift[...])
    own_rows = unit.shape[0]
    unit[...] = unit_rows[:own_rows]
    scale[...] = jnp.broadcast_to(inv_scale[:own_rows], scale.shape)
    width = normed.shape[1]
    rest = fill(rows[:, width:], width)
    normed[...] = jnp.concatenate([rows[:, :width], rest], axis=0).astype(jnp.bfloat16)


def fill(rows, width):
    empty = width - rows.shape[1]
    if not empty:
        return rows
    return jnp.concatenate([rows, jnp.zeros((rows.shape[0], empty), rows.dtype)], axis=1)


def fold_width(own_rows, vis_width):
    lines = pl.cdiv(own_rows, 8) * 8
    width = pl.cdiv(own_rows * vis_width, lines * 128) * 128
    while True:
        rest = vis_width % width
        used = own_rows * (vis_width // width) + (pl.cdiv(own_rows, width // rest) if rest else 0)
        if used <= lines:
            return lines, width
        width += 128


def pack(rows, lines, width):
    own_rows, vis_width = rows.shape
    whole = vis_width // width * width
    parts = [rows[:, first : first + width] for first in range(0, whole, width)]
    if vis_width > whole:
        beside = width // (vis_width - whole)
        for first in range(0, own_rows, beside):
            last = min(first + beside, own_rows)
            line = jnp.concatenate([rows[row : row + 1, whole:] for row in range(first, last)], axis=1)
            parts.append(fill(line, width))
    empty = lines - sum(part.shape[0] for part in parts)
    if empty:
        parts.append(jnp.zeros((empty, width), rows.dtype))
    return jnp.concatenate(parts, axis=0)


def unpack(packed, own_rows, vis_width):
    width = packed.shape[1]
    count = vis_width // width
    rest = vis_width - count * width
    parts = [packed[at * own_rows : (at + 1) * own_rows] for at in range(count)]
    if rest:
        beside, base = width // rest, count * own_rows
        parts.append(
            jnp.concatenate(
                [
                    packed[base + row // beside : base + row // beside + 1, row % beside * rest : (row % beside + 1) * rest]
                    for row in range(own_rows)
                ],
                axis=0,
            )
        )
    return jnp.concatenate(parts, axis=1)


def distance_of(place, groups):
    distance = jnp.zeros_like(place)
    step, bit = groups // 2, 1
    while step:
        distance = jnp.where((place & bit) != 0, distance + step, distance)
        step, bit = step // 2, bit * 2
    return distance


def slot_targets(my_group, own_rows, lanes, groups, img_seq, img_count, img_offset):
    group_rows = own_rows * lanes
    slots = lax.broadcasted_iota(jnp.int32, (1, group_rows * groups), 1)
    lane = slots // (own_rows * groups)
    left = slots - lane * (own_rows * groups)
    held = left // own_rows
    row_ids = (my_group ^ distance_of(held, groups)) * group_rows + (lane - held) * own_rows + left
    target = jnp.zeros_like(row_ids)
    start = jnp.int32(0)
    for image in range(img_seq.shape[0]):
        end = start + img_count[image]
        member = (row_ids >= start) & (row_ids < end)
        base = img_seq[image] * group_rows + img_offset[image] - start
        target = jnp.where(member, row_ids + base, target)
        start = end
    return target


def join_kernel(*refs):
    parts, out, first = refs[:-1], refs[-1], 0
    for part in parts:
        out[first : first + part.shape[0]] = part[...]
        first += part.shape[0]


def fetch(first, w_far, near, arrived):
    copy = pltpu.make_async_copy(w_far.at[pl.ds(first, near.shape[0])], near, arrived)
    copy.start()
    return copy


def load_all(pairs, small):
    loads = [pltpu.make_async_copy(far, close, small.at[at]) for at, (far, close) in enumerate(pairs)]
    for load in loads:
        load.start()
    return loads


def fetch_kernel(
    first, place, w_far, feats_far, grads_far, gain_far, shift_far,
    near, feats, grads, gain, shift, gain_line, shift_line, arrived, small,
):
    del place
    copy = fetch(first, w_far, near, arrived)
    pairs = ((feats_far, feats.at[0]), (grads_far, grads), (gain_far, gain_line), (shift_far, shift_line))
    for load in load_all(pairs, small):
        load.wait()
    gain[...] = gain_line[...][None]
    shift[...] = shift_line[...][None]
    copy.wait()


def fetch_and_route_kernel(
    first, own_rows, lanes, groups,
    place, img_seq_far, img_count_far, img_offset_far, bias_far, w_far, after,
    near, bias, sources, own_sources, arrivals,
    img_seq, img_count, img_offset, arrived, small,
):
    del after
    copy = fetch(first, w_far, near, arrived)
    pairs = (
        (img_seq_far, img_seq),
        (img_count_far, img_count),
        (img_offset_far, img_offset),
        (bias_far, bias),
    )
    for load in load_all(pairs, small):
        load.wait()
    group_rows = own_rows * lanes
    all_rows = group_rows * groups
    my_group = place[0]
    target = slot_targets(my_group, own_rows, lanes, groups, img_seq, img_count, img_offset)
    places = lax.broadcasted_iota(jnp.int32, (all_rows, all_rows), 0)
    held = places // group_rows
    seq_rows = places - held * group_rows + (my_group ^ distance_of(held, groups)) * group_rows
    routes = (target == seq_rows).astype(jnp.float32)
    arrivals[...] = routes[:group_rows].astype(jnp.bfloat16)
    turned = routes.T
    sources[...] = turned.astype(jnp.bfloat16)
    own_sources[...] = own_slots(turned, own_rows, lanes, groups).astype(jnp.bfloat16)
    copy.wait()


def own_slots(rows, own_rows, lanes, groups):
    stride = own_rows * groups
    return jnp.concatenate([rows[lane * stride : lane * stride + own_rows] for lane in range(lanes)], axis=0)


def terms_kernel(
    own_rows, lanes, groups, piece, packed, grads, bias, own_sources, low, high, rows, pre_act, far, terms, left
):
    stride = own_rows * groups
    held = packed[...].astype(jnp.float32)
    upper = [held[2 * lane * stride : (2 * lane + 1) * stride] for lane in range(lanes)]
    lower = [held[(2 * lane + 1) * stride : 2 * (lane + 1) * stride, : high.shape[0]] for lane in range(lanes)]
    upper = jnp.concatenate(upper, axis=0).astype(jnp.bfloat16)
    lower = jnp.concatenate(lower, axis=0).astype(jnp.bfloat16)
    rows[:, : low.shape[0]] = upper
    rows[:, low.shape[0] :] = lower
    total = bias[...] + jnp.dot(upper, low[...], preferred_element_type=jnp.float32)
    total = total + jnp.dot(lower, high[...], preferred_element_type=jnp.float32)
    pre_act[...] = total
    slope = gelu_and_slope(own_slots(total, own_rows, lanes, groups))[1]
    upstream = jnp.dot(own_sources[...], grads[...], preferred_element_type=jnp.float32)
    own = (upstream * slope).astype(jnp.bfloat16)
    pieces = []
    for part in (low, high):
        for first in range(0, part.shape[0], piece):
            weights = part[first : min(first + piece, part.shape[0])]
            left_side, right_side = (weights, own) if len(pieces) % 2 else (own, weights)
            product = lax.dot_general(
                left_side, right_side, (((1,), (1,)), ((), ())), preferred_element_type=jnp.float32
            )
            pieces.append(product.T if len(pieces) % 2 else product)
    term = jnp.concatenate(pieces, axis=1)
    copies = []
    for lane in range(lanes):
        mine = term[lane * own_rows : (lane + 1) * own_rows]
        terms[lane] = pack(mine, terms.shape[1], terms.shape[2]).astype(jnp.bfloat16)
        copies.append(pltpu.make_async_copy(terms.at[lane], far.at[lane], left.at[lane]))
        copies[-1].start()
    for copy in copies:
        copy.wait()


def grad_weight_kernel(
    height, rows, grads, pre_act, sources, arrivals, projected_far, bias_far, far,
    projected, grad_bias, grad_pre, near, left, small,
):
    acted, slope = gelu_and_slope(pre_act[...])
    upstream = jnp.dot(sources[...], grads[...], preferred_element_type=jnp.float32)
    pulled = (upstream * slope).astype(jnp.bfloat16)
    grad_pre[...] = pulled
    copies = []
    for step in range(rows.shape[1] // height):
        span = slice(step * height, (step + 1) * height)
        near[span, :] = lax.dot_general(
            rows[:, span], grad_pre[...], (((0,), (0,)), ((), ())), preferred_element_type=jnp.float32
        )
        copies.append(pltpu.make_async_copy(near.at[span], far.at[span], left.at[step]))
        copies[-1].start()
        if step == 0:
            projected[...] = jnp.dot(
                arrivals[...], acted.astype(jnp.bfloat16), preferred_element_type=jnp.float32
            ).astype(jnp.bfloat16)
            grad_bias[...] = jnp.sum(pulled.astype(jnp.float32), axis=0, keepdims=True)
            for at, (close, out) in enumerate(((projected, projected_far), (grad_bias, bias_far))):
                copies.append(pltpu.make_async_copy(close, out, small.at[at]))
                copies[-1].start()
    for copy in copies:
        copy.wait()


def finish_kernel(swapped, gain, unit, scale, grad_feats):
    total = swapped[0].astype(jnp.float32)
    for lane in range(1, swapped.shape[0]):
        total = total + swapped[lane].astype(jnp.float32)
    grad_feats[...] = backward_norm(unpack(total, *unit.shape), gain[...], unit[...], scale[:, :1])


def in_hbm(*arrays):
    return [pltpu.with_memory_space_constraint(array, pltpu.HBM) for array in arrays]


def near_call(kernel, name, outs, in_specs, operands, scratch=(), out_specs=None, moved=0, limit=24):
    return pl.pallas_call(
        kernel,
        out_shape=outs,
        in_specs=in_specs,
        out_specs=out_specs or (WHOLE,) * len(outs),
        scratch_shapes=list(scratch),
        compiler_params=pltpu.CompilerParams(vmem_limit_bytes=limit * MIB),
        cost_estimate=pl.CostEstimate(flops=0, bytes_accessed=moved, transcendentals=0),
        name=name,
    )(*operands)


def gathered_plan(feats, ln_gain, ln_shift, w_proj, b_proj, cotangent, img_seq, img_count, img_offset):
    lanes = lax.axis_size("dev")
    groups = lax.axis_size("grp")
    my_group = lax.axis_index("grp")
    own_rows, vis_width = feats.shape
    units = w_proj.shape[1]
    group_rows = own_rows * lanes
    all_rows = group_rows * groups
    half = pl.cdiv(vis_width, 256) * 128
    lines, width = fold_width(own_rows, vis_width)
    shape, bfloat16, float32 = jax.ShapeDtypeStruct, jnp.bfloat16, jnp.float32
    place = my_group[None]
    feats_far, w_far, bias_far = in_hbm(feats, w_proj, b_proj[None])

    def swap(held, step):
        return lax.ppermute(held, "grp", [(group, group ^ step) for group in range(groups)])

    def join(*parts):
        rows = sum(part.shape[0] for part in parts)
        outs = (shape((rows, *parts[0].shape[1:]), bfloat16),)
        return near_call(join_kernel, "join", outs, [WHOLE] * len(parts), parts, limit=8)[0]

    step = groups // 2
    if step:
        feats_swapped, grads_swapped = swap(feats[None], step), swap(cotangent, step)
    w_low, column, grads, gain, shift = near_call(
        functools.partial(fetch_kernel, 0),
        "fetch",
        (
            shape((half, units), bfloat16),
            shape((1, own_rows, vis_width), bfloat16),
            shape(cotangent.shape, bfloat16),
            shape((1, vis_width), float32),
            shape((1, vis_width), float32),
        ),
        [LEFT] * 6,
        (place, w_far, feats_far, *in_hbm(cotangent, ln_gain, ln_shift)),
        [
            pltpu.VMEM((vis_width,), float32),
            pltpu.VMEM((vis_width,), float32),
            pltpu.SemaphoreType.DMA,
            pltpu.SemaphoreType.DMA((4,)),
        ],
        moved=vis_width * units,
        limit=8,
    )
    blocks, later = [column], column
    while step:
        blocks = [column, feats_swapped]
        grads = join(grads, grads_swapped)
        step //= 2
        if step:
            column = later = join(*blocks)
            feats_swapped, grads_swapped = swap(column, step), swap(grads, step)
    w_high, bias, sources, own_sources, arrivals = near_call(
        functools.partial(fetch_and_route_kernel, half, own_rows, lanes, groups),
        "fetch_and_route",
        (
            shape((vis_width - half, units), bfloat16),
            shape((1, units), float32),
            shape((all_rows, all_rows), bfloat16),
            shape((group_rows, all_rows), bfloat16),
            shape((group_rows, all_rows), bfloat16),
        ),
        [SCALARS] + [LEFT] * 6,
        (place, *in_hbm(img_seq, img_count, img_offset), bias_far, w_far, later),
        [pltpu.SMEM(img_seq.shape, jnp.int32)] * 3
        + [pltpu.SemaphoreType.DMA, pltpu.SemaphoreType.DMA((4,))],
        moved=vis_width * units,
        limit=8,
    )
    column, unit, scale = near_call(
        norm_kernel,
        "norm",
        (
            shape((2 * groups * own_rows, half), bfloat16),
            shape(feats.shape, float32),
            shape((own_rows, 128), float32),
        ),
        [WHOLE] * (len(blocks) + 2),
        (*blocks, gain, shift),
        limit=8,
    )
    packed = lax.all_gather(column, "dev", axis=0, tiled=True)
    rows, pre_act, terms = near_call(
        functools.partial(terms_kernel, own_rows, lanes, groups, 256),
        "terms",
        (
            shape((all_rows, vis_width), bfloat16),
            shape((all_rows, units), float32),
            pltpu.HBM((lanes, lines, width), bfloat16),
        ),
        [WHOLE] * 6,
        (packed, grads, bias, own_sources, w_low, w_high),
        [pltpu.VMEM((lanes, lines, width), bfloat16), pltpu.SemaphoreType.DMA((lanes,))],
        (WHOLE, WHOLE, LEFT),
        moved=4 * vis_width * units,
    )
    swapped = lax.all_to_all(terms, "dev", 0, 0)
    height = 128 if vis_width % 128 == 0 else vis_width
    projected, grad_bias, grad_weight = near_call(
        functools.partial(grad_weight_kernel, height),
        "grad_weight",
        (
            pltpu.HBM((group_rows, units), bfloat16),
            pltpu.HBM((1, units), float32),
            pltpu.HBM((vis_width, units), float32),
        ),
        [WHOLE] * 5,
        (rows, grads, pre_act, sources, arrivals),
        [
            pltpu.VMEM((group_rows, units), bfloat16),
            pltpu.VMEM((1, units), float32),
            pltpu.VMEM((all_rows, units), bfloat16),
            pltpu.VMEM((vis_width, units), float32),
            pltpu.SemaphoreType.DMA((vis_width // height,)),
            pltpu.SemaphoreType.DMA((2,)),
        ],
        (LEFT,) * 3,
        moved=4 * vis_width * units,
        limit=20,
    )
    (grad_feats,) = near_call(
        finish_kernel,
        "finish",
        (shape(feats.shape, bfloat16),),
        [WHOLE] * 4,
        (swapped, gain, unit, scale),
        limit=8,
    )
    return (projected, grad_feats, grad_weight, grad_bias[0])


def summed_plan(feats, ln_gain, ln_shift, w_proj, b_proj, cotangent, img_seq, img_count, img_offset):
    lane_count = lax.axis_size("dev")
    groups = lax.axis_size("grp")
    my_group = lax.axis_index("grp")
    own_rows = feats.shape[0]
    group_rows = own_rows * lane_count
    all_rows = group_rows * groups
    row_base = my_group * group_rows
    target = row_targets(img_seq, img_count, img_offset, all_rows, group_rows)
    source_rows = (
        jnp.zeros((all_rows,), jnp.int32).at[target].set(jnp.arange(all_rows, dtype=jnp.int32))
    )
    arrivals = lax.dynamic_slice_in_dim(source_rows, row_base, group_rows)
    whole = lax.all_gather(feats, "dev", axis=0, tiled=True)
    unit_rows, inv_scale, normed = normalize(whole, ln_gain, ln_shift)
    normed = normed.astype(jnp.bfloat16)
    pre_act = jnp.dot(normed, w_proj, preferred_element_type=jnp.float32) + b_proj
    acted, slope = gelu_and_slope(pre_act)
    local_cols = acted.astype(jnp.bfloat16)
    all_cols = lax.all_gather(local_cols, "grp", axis=0, tiled=True)
    projected = all_cols[arrivals]
    all_grads = lax.all_gather(cotangent, "grp", axis=0, tiled=True)
    own_targets = lax.dynamic_slice_in_dim(target, row_base, group_rows)
    upstream = all_grads[own_targets]
    grad_pre = (upstream.astype(jnp.float32) * slope).astype(jnp.bfloat16)
    weight_term = lax.dot_general(
        normed, grad_pre, (((0,), (0,)), ((), ())), preferred_element_type=jnp.float32
    )
    bias_term = jnp.sum(grad_pre.astype(jnp.float32), axis=0)
    vis_width = weight_term.shape[0]
    padded_rows = (vis_width + groups) // groups * groups
    joint_term = jnp.concatenate(
        [
            weight_term,
            bias_term[None, :],
            jnp.zeros((padded_rows - vis_width - 1, weight_term.shape[1]), jnp.float32),
        ],
        axis=0,
    )
    summed_share = lax.psum_scatter(joint_term, "grp", scatter_dimension=0, tiled=True)
    summed_whole = lax.all_gather(
        summed_share.astype(jnp.bfloat16), "grp", axis=0, tiled=True
    ).astype(summed_share.dtype)
    grad_weight = summed_whole[:vis_width]
    grad_bias = summed_whole[vis_width]
    grad_normed = lax.psum_scatter(
        lax.dot_general(
            grad_pre, w_proj, (((1,), (1,)), ((), ())), preferred_element_type=jnp.float32
        ),
        "dev",
        scatter_dimension=0,
        tiled=True,
    )
    lane_start = lax.axis_index("dev") * own_rows
    own_unit = lax.dynamic_slice_in_dim(unit_rows, lane_start, own_rows, 0)
    own_scale = lax.dynamic_slice_in_dim(inv_scale, lane_start, own_rows, 0)
    grad_feats = backward_norm(grad_normed, ln_gain, own_unit, own_scale)
    return (projected, grad_feats, grad_weight, grad_bias)


def local(*arrays):
    feats, w_proj = arrays[0], arrays[3]
    all_rows = feats.shape[0] * lax.axis_size("dev") * lax.axis_size("grp")
    groups = lax.axis_size("grp")
    lighter = all_rows * jnp.dtype(jnp.bfloat16).itemsize <= w_proj.shape[1] * jnp.dtype(jnp.float32).itemsize
    if lighter and groups & (groups - 1) == 0:
        return gathered_plan(*arrays)
    return summed_plan(*arrays)


def solution(mesh):
    placed = (
        P(("grp", "dev"), None),
        P(),
        P(),
        P(None, "dev"),
        P("dev"),
        P("grp", "dev"),
        P(),
        P(),
        P(),
    )
    return jax.shard_map(
        local,
        mesh=mesh,
        in_specs=placed,
        out_specs=(P("grp", "dev"), P(("grp", "dev"), None), P(None, "dev"), P("dev")),
        check_vma=False,
    )
```

```python
import functools

import jax
import jax.numpy as jnp
from jax import lax
from jax.experimental import pallas as pl
from jax.experimental.pallas import tpu as pltpu
from jax.sharding import PartitionSpec as P

epsilon = 1e-05
root_two_over_pi = 0.7978845608028654
cubic = 0.044715
MIB = 1 << 20
WHOLE = pl.BlockSpec(memory_space=pltpu.VMEM)
SCALARS = pl.BlockSpec(memory_space=pltpu.SMEM)
LEFT = pl.BlockSpec(memory_space=pl.ANY)


def row_targets(img_seq, img_count, img_offset, all_rows, seq_rows):
    image_ids = jnp.arange(img_count.shape[0], dtype=jnp.int32)
    img_starts = jnp.sum(
        jnp.where(image_ids[None, :] < image_ids[:, None], img_count[None, :], 0), axis=1
    )
    img_ends = img_starts + img_count
    row_ids = jnp.arange(all_rows, dtype=jnp.int32)
    member = (
        (row_ids[:, None] >= img_starts[None, :]) & (row_ids[:, None] < img_ends[None, :])
    ).astype(jnp.int32)
    base_rows = img_seq * seq_rows + img_offset - img_starts
    return jnp.sum(member * base_rows[None, :], axis=1) + row_ids


def normalize(rows, ln_gain, ln_shift):
    values = rows.astype(jnp.float32)
    row_mean = jnp.mean(values, axis=1, keepdims=True)
    centered = values - row_mean
    inv_scale = lax.rsqrt(jnp.mean(centered * centered, axis=1, keepdims=True) + epsilon)
    unit_rows = centered * inv_scale
    return (unit_rows, inv_scale, unit_rows * ln_gain + ln_shift)


def gelu_and_slope(values):
    square = values * values
    bent = jnp.tanh(root_two_over_pi * values * (1.0 + cubic * square))
    half = 0.5 * (1.0 + bent)
    slope = half + 0.5 * values * (1.0 - bent * bent) * (
        root_two_over_pi * (1.0 + 3.0 * cubic * square)
    )
    return values * half, slope


def backward_norm(grad_normed, ln_gain, unit_rows, inv_scale):
    scaled_grad = grad_normed * ln_gain
    grad_feats = inv_scale * (
        scaled_grad
        - jnp.mean(scaled_grad, axis=1, keepdims=True)
        - unit_rows * jnp.mean(scaled_grad * unit_rows, axis=1, keepdims=True)
    )
    return grad_feats.astype(jnp.bfloat16)


def norm_kernel(*refs):
    parts, gain, shift, (normed, unit, scale) = refs[:-5], refs[-5], refs[-4], refs[-3:]
    blocks = [part[at].astype(jnp.float32) for part in parts for at in range(part.shape[0])]
    unit_rows, inv_scale, rows = normalize(jnp.concatenate(blocks, axis=0), gain[...], shift[...])
    own_rows = unit.shape[0]
    unit[...] = unit_rows[:own_rows]
    scale[...] = jnp.broadcast_to(inv_scale[:own_rows], scale.shape)
    width = normed.shape[1]
    rest = fill(rows[:, width:], width)
    normed[...] = jnp.concatenate([rows[:, :width], rest], axis=0).astype(jnp.bfloat16)


def fill(rows, width):
    empty = width - rows.shape[1]
    if not empty:
        return rows
    return jnp.concatenate([rows, jnp.zeros((rows.shape[0], empty), rows.dtype)], axis=1)


def fold_width(own_rows, vis_width):
    lines = pl.cdiv(own_rows, 8) * 8
    width = pl.cdiv(own_rows * vis_width, lines * 128) * 128
    while True:
        rest = vis_width % width
        used = own_rows * (vis_width // width) + (pl.cdiv(own_rows, width // rest) if rest else 0)
        if used <= lines:
            return lines, width
        width += 128


def pack(rows, lines, width):
    own_rows, vis_width = rows.shape
    whole = vis_width // width * width
    parts = [rows[:, first : first + width] for first in range(0, whole, width)]
    if vis_width > whole:
        beside = width // (vis_width - whole)
        for first in range(0, own_rows, beside):
            last = min(first + beside, own_rows)
            line = jnp.concatenate([rows[row : row + 1, whole:] for row in range(first, last)], axis=1)
            parts.append(fill(line, width))
    empty = lines - sum(part.shape[0] for part in parts)
    if empty:
        parts.append(jnp.zeros((empty, width), rows.dtype))
    return jnp.concatenate(parts, axis=0)


def unpack(packed, own_rows, vis_width):
    width = packed.shape[1]
    count = vis_width // width
    rest = vis_width - count * width
    parts = [packed[at * own_rows : (at + 1) * own_rows] for at in range(count)]
    if rest:
        beside, base = width // rest, count * own_rows
        parts.append(
            jnp.concatenate(
                [
                    packed[base + row // beside : base + row // beside + 1, row % beside * rest : (row % beside + 1) * rest]
                    for row in range(own_rows)
                ],
                axis=0,
            )
        )
    return jnp.concatenate(parts, axis=1)


def distance_of(place, groups):
    distance = jnp.zeros_like(place)
    step, bit = groups // 2, 1
    while step:
        distance = jnp.where((place & bit) != 0, distance + step, distance)
        step, bit = step // 2, bit * 2
    return distance


def slot_targets(my_group, own_rows, lanes, groups, img_seq, img_count, img_offset):
    group_rows = own_rows * lanes
    slots = lax.broadcasted_iota(jnp.int32, (1, group_rows * groups), 1)
    lane = slots // (own_rows * groups)
    left = slots - lane * (own_rows * groups)
    held = left // own_rows
    row_ids = (my_group ^ distance_of(held, groups)) * group_rows + (lane - held) * own_rows + left
    target = jnp.zeros_like(row_ids)
    start = jnp.int32(0)
    for image in range(img_seq.shape[0]):
        end = start + img_count[image]
        member = (row_ids >= start) & (row_ids < end)
        base = img_seq[image] * group_rows + img_offset[image] - start
        target = jnp.where(member, row_ids + base, target)
        start = end
    return target


def join_kernel(*refs):
    parts, out, first = refs[:-1], refs[-1], 0
    for part in parts:
        out[first : first + part.shape[0]] = part[...]
        first += part.shape[0]


def fetch(first, w_far, near, arrived):
    copy = pltpu.make_async_copy(w_far.at[pl.ds(first, near.shape[0])], near, arrived)
    copy.start()
    return copy


def load_all(pairs, small):
    loads = [pltpu.make_async_copy(far, close, small.at[at]) for at, (far, close) in enumerate(pairs)]
    for load in loads:
        load.start()
    return loads


def fetch_kernel(
    first, place, w_far, feats_far, grads_far, gain_far, shift_far,
    near, feats, grads, gain, shift, gain_line, shift_line, arrived, small,
):
    del place
    copy = fetch(first, w_far, near, arrived)
    pairs = ((feats_far, feats.at[0]), (grads_far, grads), (gain_far, gain_line), (shift_far, shift_line))
    for load in load_all(pairs, small):
        load.wait()
    gain[...] = gain_line[...][None]
    shift[...] = shift_line[...][None]
    copy.wait()


def fetch_and_route_kernel(
    first, own_rows, lanes, groups,
    place, img_seq_far, img_count_far, img_offset_far, bias_far, w_far, after,
    near, bias, sources, own_sources, arrivals,
    img_seq, img_count, img_offset, arrived, small,
):
    del after
    copy = fetch(first, w_far, near, arrived)
    pairs = (
        (img_seq_far, img_seq),
        (img_count_far, img_count),
        (img_offset_far, img_offset),
        (bias_far, bias),
    )
    for load in load_all(pairs, small):
        load.wait()
    group_rows = own_rows * lanes
    all_rows = group_rows * groups
    my_group = place[0]
    target = slot_targets(my_group, own_rows, lanes, groups, img_seq, img_count, img_offset)
    places = lax.broadcasted_iota(jnp.int32, (all_rows, all_rows), 0)
    held = places // group_rows
    seq_rows = places - held * group_rows + (my_group ^ distance_of(held, groups)) * group_rows
    routes = (target == seq_rows).astype(jnp.float32)
    arrivals[...] = routes[:group_rows].astype(jnp.bfloat16)
    turned = routes.T
    sources[...] = turned.astype(jnp.bfloat16)
    own_sources[...] = own_slots(turned, own_rows, lanes, groups).astype(jnp.bfloat16)
    copy.wait()


def own_slots(rows, own_rows, lanes, groups):
    stride = own_rows * groups
    return jnp.concatenate([rows[lane * stride : lane * stride + own_rows] for lane in range(lanes)], axis=0)


def terms_kernel(
    own_rows, lanes, groups, piece, packed, grads, bias, own_sources, low, high, rows, pre_act, far, terms, left
):
    stride = own_rows * groups
    held = packed[...].astype(jnp.float32)
    upper = [held[2 * lane * stride : (2 * lane + 1) * stride] for lane in range(lanes)]
    lower = [held[(2 * lane + 1) * stride : 2 * (lane + 1) * stride, : high.shape[0]] for lane in range(lanes)]
    upper = jnp.concatenate(upper, axis=0).astype(jnp.bfloat16)
    lower = jnp.concatenate(lower, axis=0).astype(jnp.bfloat16)
    rows[:, : low.shape[0]] = upper
    rows[:, low.shape[0] :] = lower
    total = bias[...] + jnp.dot(upper, low[...], preferred_element_type=jnp.float32)
    total = total + jnp.dot(lower, high[...], preferred_element_type=jnp.float32)
    pre_act[...] = total
    slope = gelu_and_slope(own_slots(total, own_rows, lanes, groups))[1]
    upstream = jnp.dot(own_sources[...], grads[...], preferred_element_type=jnp.float32)
    own = (upstream * slope).astype(jnp.bfloat16)
    pieces = []
    for part in (low, high):
        for first in range(0, part.shape[0], piece):
            weights = part[first : min(first + piece, part.shape[0])]
            left_side, right_side = (own, weights) if len(pieces) % 2 else (weights, own)
            product = lax.dot_general(
                left_side, right_side, (((1,), (1,)), ((), ())), preferred_element_type=jnp.float32
            )
            pieces.append(product if len(pieces) % 2 else product.T)
    term = jnp.concatenate(pieces, axis=1)
    copies = []
    for lane in range(lanes):
        mine = term[lane * own_rows : (lane + 1) * own_rows]
        terms[lane] = pack(mine, terms.shape[1], terms.shape[2]).astype(jnp.bfloat16)
        copies.append(pltpu.make_async_copy(terms.at[lane], far.at[lane], left.at[lane]))
        copies[-1].start()
    for copy in copies:
        copy.wait()


def grad_weight_kernel(
    height, rows, grads, pre_act, sources, arrivals, projected_far, bias_far, far,
    projected, grad_bias, grad_pre, near, left, small,
):
    acted, slope = gelu_and_slope(pre_act[...])
    upstream = jnp.dot(sources[...], grads[...], preferred_element_type=jnp.float32)
    pulled = (upstream * slope).astype(jnp.bfloat16)
    grad_pre[...] = pulled
    copies = []
    for step in range(rows.shape[1] // height):
        span = slice(step * height, (step + 1) * height)
        near[span, :] = lax.dot_general(
            rows[:, span], grad_pre[...], (((0,), (0,)), ((), ())), preferred_element_type=jnp.float32
        )
        copies.append(pltpu.make_async_copy(near.at[span], far.at[span], left.at[step]))
        copies[-1].start()
        if step == 0:
            projected[...] = jnp.dot(
                arrivals[...], acted.astype(jnp.bfloat16), preferred_element_type=jnp.float32
            ).astype(jnp.bfloat16)
            grad_bias[...] = jnp.sum(pulled.astype(jnp.float32), axis=0, keepdims=True)
            for at, (close, out) in enumerate(((projected, projected_far), (grad_bias, bias_far))):
                copies.append(pltpu.make_async_copy(close, out, small.at[at]))
                copies[-1].start()
    for copy in copies:
        copy.wait()


def finish_kernel(swapped, gain, unit, scale, grad_feats):
    total = swapped[0].astype(jnp.float32)
    for lane in range(1, swapped.shape[0]):
        total = total + swapped[lane].astype(jnp.float32)
    grad_feats[...] = backward_norm(unpack(total, *unit.shape), gain[...], unit[...], scale[:, :1])


def in_hbm(*arrays):
    return [pltpu.with_memory_space_constraint(array, pltpu.HBM) for array in arrays]


def near_call(kernel, name, outs, in_specs, operands, scratch=(), out_specs=None, moved=0, limit=24):
    return pl.pallas_call(
        kernel,
        out_shape=outs,
        in_specs=in_specs,
        out_specs=out_specs or (WHOLE,) * len(outs),
        scratch_shapes=list(scratch),
        compiler_params=pltpu.CompilerParams(vmem_limit_bytes=limit * MIB),
        cost_estimate=pl.CostEstimate(flops=0, bytes_accessed=moved, transcendentals=0),
        name=name,
    )(*operands)


def gathered_plan(feats, ln_gain, ln_shift, w_proj, b_proj, cotangent, img_seq, img_count, img_offset):
    lanes = lax.axis_size("dev")
    groups = lax.axis_size("grp")
    my_group = lax.axis_index("grp")
    own_rows, vis_width = feats.shape
    units = w_proj.shape[1]
    group_rows = own_rows * lanes
    all_rows = group_rows * groups
    half = pl.cdiv(vis_width, 256) * 128
    lines, width = fold_width(own_rows, vis_width)
    shape, bfloat16, float32 = jax.ShapeDtypeStruct, jnp.bfloat16, jnp.float32
    place = my_group[None]
    feats_far, w_far, bias_far = in_hbm(feats, w_proj, b_proj[None])

    def swap(held, step):
        return lax.ppermute(held, "grp", [(group, group ^ step) for group in range(groups)])

    def join(*parts):
        rows = sum(part.shape[0] for part in parts)
        outs = (shape((rows, *parts[0].shape[1:]), bfloat16),)
        return near_call(join_kernel, "join", outs, [WHOLE] * len(parts), parts, limit=8)[0]

    step = groups // 2
    if step:
        feats_swapped, grads_swapped = swap(feats[None], step), swap(cotangent, step)
    w_low, column, grads, gain, shift = near_call(
        functools.partial(fetch_kernel, 0),
        "fetch",
        (
            shape((half, units), bfloat16),
            shape((1, own_rows, vis_width), bfloat16),
            shape(cotangent.shape, bfloat16),
            shape((1, vis_width), float32),
            shape((1, vis_width), float32),
        ),
        [LEFT] * 6,
        (place, w_far, feats_far, *in_hbm(cotangent, ln_gain, ln_shift)),
        [
            pltpu.VMEM((vis_width,), float32),
            pltpu.VMEM((vis_width,), float32),
            pltpu.SemaphoreType.DMA,
            pltpu.SemaphoreType.DMA((4,)),
        ],
        moved=vis_width * units,
        limit=8,
    )
    blocks, later = [column], column
    while step:
        blocks = [column, feats_swapped]
        grads = join(grads, grads_swapped)
        step //= 2
        if step:
            column = later = join(*blocks)
            feats_swapped, grads_swapped = swap(column, step), swap(grads, step)
    w_high, bias, sources, own_sources, arrivals = near_call(
        functools.partial(fetch_and_route_kernel, half, own_rows, lanes, groups),
        "fetch_and_route",
        (
            shape((vis_width - half, units), bfloat16),
            shape((1, units), float32),
            shape((all_rows, all_rows), bfloat16),
            shape((group_rows, all_rows), bfloat16),
            shape((group_rows, all_rows), bfloat16),
        ),
        [SCALARS] + [LEFT] * 6,
        (place, *in_hbm(img_seq, img_count, img_offset), bias_far, w_far, later),
        [pltpu.SMEM(img_seq.shape, jnp.int32)] * 3
        + [pltpu.SemaphoreType.DMA, pltpu.SemaphoreType.DMA((4,))],
        moved=vis_width * units,
        limit=8,
    )
    column, unit, scale = near_call(
        norm_kernel,
        "norm",
        (
            shape((2 * groups * own_rows, half), bfloat16),
            shape(feats.shape, float32),
            shape((own_rows, 128), float32),
        ),
        [WHOLE] * (len(blocks) + 2),
        (*blocks, gain, shift),
        limit=8,
    )
    packed = lax.all_gather(column, "dev", axis=0, tiled=True)
    rows, pre_act, terms = near_call(
        functools.partial(terms_kernel, own_rows, lanes, groups, 256),
        "terms",
        (
            shape((all_rows, vis_width), bfloat16),
            shape((all_rows, units), float32),
            pltpu.HBM((lanes, lines, width), bfloat16),
        ),
        [WHOLE] * 6,
        (packed, grads, bias, own_sources, w_low, w_high),
        [pltpu.VMEM((lanes, lines, width), bfloat16), pltpu.SemaphoreType.DMA((lanes,))],
        (WHOLE, WHOLE, LEFT),
        moved=4 * vis_width * units,
    )
    swapped = lax.all_to_all(terms, "dev", 0, 0)
    height = 128 if vis_width % 128 == 0 else vis_width
    projected, grad_bias, grad_weight = near_call(
        functools.partial(grad_weight_kernel, height),
        "grad_weight",
        (
            pltpu.HBM((group_rows, units), bfloat16),
            pltpu.HBM((1, units), float32),
            pltpu.HBM((vis_width, units), float32),
        ),
        [WHOLE] * 5,
        (rows, grads, pre_act, sources, arrivals),
        [
            pltpu.VMEM((group_rows, units), bfloat16),
            pltpu.VMEM((1, units), float32),
            pltpu.VMEM((all_rows, units), bfloat16),
            pltpu.VMEM((vis_width, units), float32),
            pltpu.SemaphoreType.DMA((vis_width // height,)),
            pltpu.SemaphoreType.DMA((2,)),
        ],
        (LEFT,) * 3,
        moved=4 * vis_width * units,
        limit=20,
    )
    (grad_feats,) = near_call(
        finish_kernel,
        "finish",
        (shape(feats.shape, bfloat16),),
        [WHOLE] * 4,
        (swapped, gain, unit, scale),
        limit=8,
    )
    return (projected, grad_feats, grad_weight, grad_bias[0])


def summed_plan(feats, ln_gain, ln_shift, w_proj, b_proj, cotangent, img_seq, img_count, img_offset):
    lane_count = lax.axis_size("dev")
    groups = lax.axis_size("grp")
    my_group = lax.axis_index("grp")
    own_rows = feats.shape[0]
    group_rows = own_rows * lane_count
    all_rows = group_rows * groups
    row_base = my_group * group_rows
    target = row_targets(img_seq, img_count, img_offset, all_rows, group_rows)
    source_rows = (
        jnp.zeros((all_rows,), jnp.int32).at[target].set(jnp.arange(all_rows, dtype=jnp.int32))
    )
    arrivals = lax.dynamic_slice_in_dim(source_rows, row_base, group_rows)
    whole = lax.all_gather(feats, "dev", axis=0, tiled=True)
    unit_rows, inv_scale, normed = normalize(whole, ln_gain, ln_shift)
    normed = normed.astype(jnp.bfloat16)
    pre_act = jnp.dot(normed, w_proj, preferred_element_type=jnp.float32) + b_proj
    acted, slope = gelu_and_slope(pre_act)
    local_cols = acted.astype(jnp.bfloat16)
    all_cols = lax.all_gather(local_cols, "grp", axis=0, tiled=True)
    projected = all_cols[arrivals]
    all_grads = lax.all_gather(cotangent, "grp", axis=0, tiled=True)
    own_targets = lax.dynamic_slice_in_dim(target, row_base, group_rows)
    upstream = all_grads[own_targets]
    grad_pre = (upstream.astype(jnp.float32) * slope).astype(jnp.bfloat16)
    weight_term = lax.dot_general(
        normed, grad_pre, (((0,), (0,)), ((), ())), preferred_element_type=jnp.float32
    )
    bias_term = jnp.sum(grad_pre.astype(jnp.float32), axis=0)
    vis_width = weight_term.shape[0]
    padded_rows = (vis_width + groups) // groups * groups
    joint_term = jnp.concatenate(
        [
            weight_term,
            bias_term[None, :],
            jnp.zeros((padded_rows - vis_width - 1, weight_term.shape[1]), jnp.float32),
        ],
        axis=0,
    )
    summed_share = lax.psum_scatter(joint_term, "grp", scatter_dimension=0, tiled=True)
    summed_whole = lax.all_gather(
        summed_share.astype(jnp.bfloat16), "grp", axis=0, tiled=True
    ).astype(summed_share.dtype)
    grad_weight = summed_whole[:vis_width]
    grad_bias = summed_whole[vis_width]
    grad_normed = lax.psum_scatter(
        lax.dot_general(
            grad_pre, w_proj, (((1,), (1,)), ((), ())), preferred_element_type=jnp.float32
        ),
        "dev",
        scatter_dimension=0,
        tiled=True,
    )
    lane_start = lax.axis_index("dev") * own_rows
    own_unit = lax.dynamic_slice_in_dim(unit_rows, lane_start, own_rows, 0)
    own_scale = lax.dynamic_slice_in_dim(inv_scale, lane_start, own_rows, 0)
    grad_feats = backward_norm(grad_normed, ln_gain, own_unit, own_scale)
    return (projected, grad_feats, grad_weight, grad_bias)


def local(*arrays):
    feats, w_proj = arrays[0], arrays[3]
    all_rows = feats.shape[0] * lax.axis_size("dev") * lax.axis_size("grp")
    groups = lax.axis_size("grp")
    lighter = all_rows * jnp.dtype(jnp.bfloat16).itemsize <= w_proj.shape[1] * jnp.dtype(jnp.float32).itemsize
    if lighter and groups & (groups - 1) == 0:
        return gathered_plan(*arrays)
    return summed_plan(*arrays)


def solution(mesh):
    placed = (
        P(("grp", "dev"), None),
        P(),
        P(),
        P(None, "dev"),
        P("dev"),
        P("grp", "dev"),
        P(),
        P(),
        P(),
    )
    return jax.shard_map(
        local,
        mesh=mesh,
        in_specs=placed,
        out_specs=(P("grp", "dev"), P(("grp", "dev"), None), P(None, "dev"), P("dev")),
        check_vma=False,
    )
```
